256 devices in a mesh: row: 32 (over y_hi, z, core), col: 8 (over x, y_lo).
Axes of the slice: x: 4, y: 4 (y_hi: 2, y_lo: 2; y = y_hi * 2 + y_lo), z: 8, core: 2. Of those that a mesh axis runs over, the one named last changes fastest.
Arguments:
- markers: bfloat16 [32768, 16384], P('row', 'col'), may hold values from -6 to 6
Outputs:
- solved_panel: float32 [1024, 32768], P('col', 'row')
The draws below stay inside these ranges and needn't reach their ends.
All inputs are finite; a program needn't handle non-finite values.
Results may differ from the reference program's by a relative error of at most 0.00065.
Values may be sent and summed in bfloat16 or wider, within the bound.
A program may use at most 128 MiB of HBM per device.

```python
import math
import jax
import jax.numpy as jnp
from jax import lax

M = 16384
PANEL = 1024
ROWS_DEV = 1024
PB = 32
N = 32768
N_ROW = 32


def draw_markers(key, part):
    key = jax.random.fold_in(key, 7)
    base_key, fresh_key = jax.random.split(key, 2)
    base_values = jax.random.normal(base_key, (N, M), jnp.float32)
    spread = 0.03
    clone_ids = jnp.arange(PANEL // 4, dtype=jnp.int32) * 4 + 1
    twin_ids = clone_ids - 1
    clone_rows = clone_ids // PB * ROWS_DEV + clone_ids % PB
    twin_rows = twin_ids // PB * ROWS_DEV + twin_ids % PB
    fresh_noise = jax.random.normal(fresh_key, (PANEL // 4, M), jnp.float32)
    copies = math.sqrt(1.0 - spread * spread) * base_values[twin_rows] + spread * fresh_noise
    values = base_values.at[clone_rows].set(copies)
    return jnp.clip(values, -6.0, 6.0).astype(jnp.bfloat16)


def setup_inputs(seed: int = 0) -> dict:
    arg_keys = jax.random.split(jax.random.key(seed), 2)
    return {
        "markers": draw_markers(jax.random.fold_in(arg_keys[1], 71), 0),
    }


def reference(markers):
    panel_markers = markers.reshape(N_ROW, ROWS_DEV, M)[:, :PB].reshape(PANEL, M)
    gram = lax.dot_general(panel_markers.astype(jnp.float32), markers.astype(jnp.float32), (((1,), (1,)), ((), ())), preferred_element_type=jnp.float32)
    gram = gram * (1.0 / M)
    ranks = jnp.arange(PANEL, dtype=jnp.int32)
    person = ranks // PB * ROWS_DEV + ranks % PB
    columns = jnp.arange(N, dtype=jnp.int32)
    gram = gram + jnp.where(person[:, None] == columns[None, :], 0.001, 0.0).astype(jnp.float32)
    diag_block = gram.reshape(PANEL, N_ROW, ROWS_DEV)[:, :, :PB].reshape(PANEL, PANEL)
    factor = jnp.linalg.cholesky(diag_block)
    identity = jnp.eye(PANEL, dtype=diag_block.dtype)
    inverse = lax.linalg.triangular_solve(factor, identity, left_side=True, lower=True)
    return jnp.dot(inverse, gram, precision=lax.Precision.HIGHEST)
```

```python
import functools

import jax
import jax.numpy as jnp
from jax import lax
from jax.experimental import pallas as pl
from jax.experimental.pallas import tpu as pltpu
from jax.sharding import PartitionSpec as P

M = 16384
PANEL = 1024
PB = 32
NB = 8
BK = 128
RIDGE = 0.001
MESH = pl.DeviceIdType.MESH
F32 = jnp.float32
BF16 = jnp.bfloat16


def split3(x):
    high = x.astype(BF16)
    rest = x - high.astype(F32)
    mid = rest.astype(BF16)
    low = (rest - mid.astype(F32)).astype(BF16)
    return high, mid, low


def stack_left(x, axis=1):
    high, mid, low = split3(x)
    return jnp.concatenate([high, high, high, mid, mid, low], axis=axis)


def stack_right(x, axis=1):
    high, mid, low = split3(x)
    return jnp.concatenate([high, mid, low, high, mid, high], axis=axis)


def dot_nt(a, b):
    return lax.dot_general(a, b, (((1,), (1,)), ((), ())), preferred_element_type=F32)


def dot_nn(a, b):
    return lax.dot_general(a, b, (((1,), (0,)), ((), ())), preferred_element_type=F32)


def recip(x):
    return pltpu.reciprocal(x, approx=True)


def row_of(x, i):
    return jnp.broadcast_to(x[i : i + 1, :], (8, BK))


def col_of(x, j):
    return jnp.broadcast_to(x[:, j : j + 1], (8, BK))


def factor8(c):
    w = [[None] * 8 for _ in range(8)]
    rp = [None] * 8
    for i in range(8):
        w[i][i] = jnp.ones_like(c[0][0])
    for s in range(8):
        rp[s] = recip(c[s][s])
        for i in range(s + 1, 8):
            f = c[i][s] * rp[s]
            for j in range(s + 1, i + 1):
                c[i][j] = c[i][j] - f * c[j][s]
            for q in range(s):
                w[i][q] = w[i][q] - f * w[s][q]
            w[i][s] = -f
    return w, rp


def factor_inverse(a):
    tiles = [a[8 * t : 8 * t + 8, :] for t in range(16)]
    lane = lax.broadcasted_iota(jnp.int32, (8, BK), 1)
    sub = lax.broadcasted_iota(jnp.int32, (8, BK), 0)
    out = []
    for t in range(16):
        x, b0 = tiles[t], 8 * t
        cols = [col_of(x, b0 + j) for j in range(8)]
        w, rp = factor8([[row_of(cols[j], i) for j in range(i + 1)] for i in range(8)])
        inside = (lane >= b0) & (lane < b0 + 8)
        xt = jnp.where(inside, (lane - b0 == sub).astype(F32), x)
        r = [row_of(xt, i) for i in range(8)]
        u = []
        for s in range(8):
            y = r[s]
            for j in range(s):
                y = y + w[s][j] * r[j]
            u.append(y)
        y, p = u[0], rp[0]
        for s in range(1, 8):
            y = jnp.where(sub == s, u[s], y)
            p = jnp.where(sub == s, rp[s], p)
        out.append(jnp.where(lane <= b0 + sub, y * lax.sqrt(p), 0.0))
        for i in range(t + 1, 16):
            e = [col_of(tiles[i], b0 + j) for j in range(8)]
            z = jnp.where(inside, 0.0, tiles[i])
            for s in range(8):
                f = e[s]
                for j in range(s):
                    f = f + w[s][j] * e[j]
                z = z - (f * rp[s]) * u[s]
            tiles[i] = z
    return jnp.concatenate(out, axis=0)


def cholesky_panels(a_ref, inv_ref, left_ref, right_ref):
    rows = lax.broadcasted_iota(jnp.int32, (PANEL, BK), 0)

    def step(k, carry):
        here = pl.ds(pl.multiple_of(k * BK, BK), BK)
        inverse = factor_inverse(a_ref[here, here])
        inv_ref[k] = inverse
        panel = dot_nt(stack_left(a_ref[:, here]), stack_right(inverse))
        panel = jnp.where(rows >= (k + 1) * BK, panel, 0.0)
        a_ref[:, here] = panel
        left_ref[...] = stack_left(panel)
        right_ref[...] = stack_right(panel)

        def update(j, inner):
            cols = pl.ds(pl.multiple_of(j * 2 * BK, 2 * BK), 2 * BK)
            a_ref[:, cols] -= jnp.where(
                lax.broadcasted_iota(jnp.int32, (PANEL, 2 * BK), 1) + j * 2 * BK >= (k + 1) * BK,
                dot_nt(left_ref[...], right_ref[cols, :]),
                0.0,
            )
            return inner

        lax.fori_loop((k + 1) // 2, NB // 2, update, 0)
        return carry

    lax.fori_loop(0, NB, step, 0)


def kernel(
    markers_ref, out_ref,
    own, panel, a_ref, dpart, drecv, dred, gsend, grecv, solved, inv_ref, left_ref, right_ref,
    local_sem, ag_send, ag_recv, dag_send, dag_recv, rs_send, rs_recv, dc_send, dc_recv,
    gs_send, gs_recv, os_send, os_recv,
):
    row = lax.axis_index("row")
    col = lax.axis_index("col")
    core = lax.rem(row, 2)
    z = lax.rem(row // 2, 8)
    hi = row // 16

    def row_id(h, zz, q):
        return h * 16 + zz * 2 + q

    sibling = row_id(hi, z, 1 - core)
    partner = row_id(1 - hi, z, core)
    up = row_id(hi, lax.rem(z + 1, 8), core)
    down = row_id(hi, lax.rem(z + 7, 8), core)
    row_peers = (sibling, partner, up, down)
    col_peers = [lax.rem(col + o, NB) for o in range(1, NB)]

    load_panel = pltpu.make_async_copy(
        markers_ref.at[pl.ds(0, PB), :], panel.at[pl.ds(pl.multiple_of(row * PB, PB), PB), :], local_sem.at[0]
    )
    load_panel.start()
    load_own = pltpu.make_async_copy(markers_ref, own, local_sem.at[1])
    load_own.start()

    barrier = pltpu.get_barrier_semaphore()
    for peer in row_peers:
        pl.semaphore_signal(barrier, inc=1, device_id=(peer, col), device_id_type=MESH)
    for peer in col_peers:
        pl.semaphore_signal(barrier, inc=1, device_id=(row, peer), device_id_type=MESH)
    pl.semaphore_wait(barrier, len(row_peers) + len(col_peers))

    def gather(buf, send, recv, between):
        def block(r):
            return buf.at[pl.ds(pl.multiple_of(r * PB, PB), PB), :]

        started = []

        def copy(r, target, index, go=True):
            c = pltpu.make_async_remote_copy(
                src_ref=block(r), dst_ref=block(r), send_sem=send.at[index], recv_sem=recv.at[index],
                device_id=(target, col), device_id_type=MESH,
            )
            if go:
                c.start()
                started.append(c)
            return c

        def index_of(stream, way, d):
            return (stream * 2 + way) * 4 + d - 1

        def source(stream, way, d):
            h = hi if stream == 0 else 1 - hi
            zz = lax.rem(z + (8 - d if way == 0 else d), 8)
            return row_id(h, zz, core)

        def forward(stream, way, d):
            copy(source(stream, way, d), up if way == 0 else down, index_of(stream, way, d + 1))

        reach = {(0, 0): 4, (0, 1): 3, (1, 0): 3, (1, 1): 4}
        sib = 16
        own_r = row
        part_r = partner
        copy(own_r, partner, 32)
        forward(0, 0, 0)
        forward(0, 1, 0)
        copy(own_r, sibling, sib + 0)
        between(0)
        copy(part_r, partner, 32, go=False).wait_recv()
        forward(1, 0, 0)
        forward(1, 1, 0)
        copy(part_r, sibling, sib + 1)
        n = 2
        sib_sources = [row_id(hi, z, 1 - core), row_id(1 - hi, z, 1 - core)]
        between(1)
        for d in range(1, 5):
            for stream in (0, 1):
                for way in (0, 1):
                    if d > reach[stream, way]:
                        continue
                    r = source(stream, way, d)
                    copy(r, sibling, index_of(stream, way, d), go=False).wait_recv()
                    if d < reach[stream, way]:
                        forward(stream, way, d)
                    copy(r, sibling, sib + n)
                    sib_sources.append(r + 1 - 2 * core)
                    n += 1
            between(d + 1)
        for i, r in enumerate(sib_sources):
            copy(r, sibling, sib + i, go=False).wait_recv()
        return started

    load_panel.wait()
    started = gather(panel, ag_send, ag_recv, lambda s: None)

    mine = pl.ds(pl.multiple_of(row * PB, PB), PB)
    dpart[...] = dot_nt(panel[mine, :], panel[...])

    def reduce_copy(o, target):
        return pltpu.make_async_remote_copy(
            src_ref=dpart.at[:, pl.ds(pl.multiple_of(target * BK, BK), BK)], dst_ref=drecv.at[o],
            send_sem=rs_send.at[o], recv_sem=rs_recv.at[o], device_id=(row, target), device_id_type=MESH,
        )

    scatter = [reduce_copy(o, col_peers[o - 1]) for o in range(1, NB)]
    for c in scatter:
        c.start()
    load_own.wait()
    parity = lax.rem(col, 2)

    def gram_pair(i):
        pair = lax.rem(col // 2 + i, NB // 2)
        both = dot_nt(panel[...], own[pl.ds(pl.multiple_of(pair * 2 * BK, 2 * BK), 2 * BK), :])
        gsend[2 * i + parity] = both[:, :BK]
        gsend[2 * i + 1 - parity] = both[:, BK:]

    gram_pair(1)
    for c in scatter:
        c.wait_recv()
    here = pl.ds(pl.multiple_of(col * BK, BK), BK)
    total = dpart[:, here]
    for o in range(1, NB):
        total = total + drecv[o]
    diagonal = (
        lax.broadcasted_iota(jnp.int32, (PB, BK), 0) + row * PB
        == lax.broadcasted_iota(jnp.int32, (PB, BK), 1) + col * BK
    )
    dred[...] = total * (1.0 / M) + jnp.where(diagonal, RIDGE, 0.0)
    a_ref[mine, here] = dred[...]

    def spread_copy(o, target):
        return pltpu.make_async_remote_copy(
            src_ref=dred, dst_ref=a_ref.at[mine, here],
            send_sem=dc_send.at[o], recv_sem=dc_recv.at[o], device_id=(row, target), device_id_type=MESH,
        )

    spread = [spread_copy(o, col_peers[o - 1]) for o in range(1, NB)]
    for c in spread:
        c.start()
    gram_pair(2)
    for c in spread:
        c.wait_recv()

    gram_copies = []

    def gram_copy(i, same):
        target = 2 * lax.rem(col // 2 + i, NB // 2) + (parity if same else 1 - parity)
        slot = 2 * i + (0 if same else 1)
        c = pltpu.make_async_remote_copy(
            src_ref=gsend.at[slot], dst_ref=grecv.at[slot],
            send_sem=gs_send.at[slot], recv_sem=gs_recv.at[slot], device_id=(row, target), device_id_type=MESH,
        )
        c.start()
        gram_copies.append(c)

    def between(s):
        if s == 0:
            gram_pair(3)
        elif s == 1:
            for i in (1, 2, 3):
                gram_copy(i, True)
                gram_copy(i, False)
            gram_pair(0)
            gram_copy(0, False)

    started += gather(a_ref, dag_send, dag_recv, between)

    for c in started + scatter + spread:
        c.wait_send()
    cholesky_panels(a_ref, inv_ref, left_ref, right_ref)

    for c in gram_copies:
        c.wait()
    total = gsend[0]
    for s in range(1, NB):
        total = total + grecv[s]
    ridge = (
        (lax.broadcasted_iota(jnp.int32, (PANEL, BK), 0) == lax.broadcasted_iota(jnp.int32, (PANEL, BK), 1) + row * PB)
        & (lax.broadcasted_iota(jnp.int32, (PANEL, BK), 1) < PB)
        & (col == 0)
    )
    solved[...] = total * (1.0 / M) + jnp.where(ridge, RIDGE, 0.0)

    def out_copy(k, source):
        return pltpu.make_async_remote_copy(
            src_ref=solved.at[pl.ds(k * BK, BK), :], dst_ref=out_ref.at[:, pl.ds(pl.multiple_of(source * BK, BK), BK)],
            send_sem=os_send.at[k], recv_sem=os_recv.at[source], device_id=(row, k), device_id_type=MESH,
        )

    for k in range(NB):
        s_k = dot_nn(stack_left(inv_ref[k]), stack_right(solved[k * BK : (k + 1) * BK, :], axis=0))
        solved[k * BK : (k + 1) * BK, :] = s_k

        @pl.when(col != k)
        def _():
            out_copy(k, col).start()

        @pl.when(col == k)
        def _():
            out_ref[:, here] = s_k

        if k < NB - 1:
            rest = slice((k + 1) * BK, PANEL)
            solved[rest, :] -= dot_nn(
                stack_left(a_ref[rest, k * BK : (k + 1) * BK]), stack_right(s_k, axis=0)
            )
    for k in range(NB):
        @pl.when(col != k)
        def _():
            out_copy(k, col).wait_send()
            out_copy(k, jnp.int32(k)).wait_recv()


def shards(markers):
    sem = pltpu.SemaphoreType.DMA
    return pl.pallas_call(
        kernel,
        out_shape=jax.ShapeDtypeStruct((BK, 1024), F32),
        in_specs=[pl.BlockSpec(memory_space=pl.ANY)],
        out_specs=pl.BlockSpec(memory_space=pltpu.VMEM),
        scratch_shapes=[
            pltpu.VMEM((1024, 2048), BF16),
            pltpu.VMEM((PANEL, 2048), BF16),
            pltpu.VMEM((PANEL, PANEL), F32),
            pltpu.VMEM((PB, PANEL), F32),
            pltpu.VMEM((NB, PB, BK), F32),
            pltpu.VMEM((PB, BK), F32),
            pltpu.VMEM((NB, PANEL, BK), F32),
            pltpu.VMEM((NB, PANEL, BK), F32),
            pltpu.VMEM((PANEL, BK), F32),
            pltpu.VMEM((NB, BK, BK), F32),
            pltpu.VMEM((PANEL, 6 * BK), BF16),
            pltpu.VMEM((PANEL, 6 * BK), BF16),
            sem((2,)), sem((33,)), sem((33,)), sem((33,)), sem((33,)),
            sem((NB,)), sem((NB,)), sem((NB,)), sem((NB,)),
            sem((NB,)), sem((NB,)), sem((NB,)), sem((NB,)),
        ],
        compiler_params=pltpu.CompilerParams(
            collective_id=0, has_side_effects=True, vmem_limit_bytes=58 * 1024 * 1024
        ),
    )(markers)


def solution(mesh):
    return jax.shard_map(
        shards, mesh=mesh, in_specs=(P("row", "col"),), out_specs=P("col", "row"), check_vma=False
    )
```

```python
import functools

import jax
import jax.numpy as jnp
from jax import lax
from jax.experimental import pallas as pl
from jax.experimental.pallas import tpu as pltpu
from jax.sharding import PartitionSpec as P

M = 16384
PANEL = 1024
PB = 32
NB = 8
BK = 128
RIDGE = 0.001
MESH = pl.DeviceIdType.MESH
F32 = jnp.float32
BF16 = jnp.bfloat16


def split3(x):
    high = x.astype(BF16)
    rest = x - high.astype(F32)
    mid = rest.astype(BF16)
    low = (rest - mid.astype(F32)).astype(BF16)
    return high, mid, low


def stack_left(x, axis=1):
    high, mid, low = split3(x)
    return jnp.concatenate([high, high, high, mid, mid, low], axis=axis)


def stack_right(x, axis=1):
    high, mid, low = split3(x)
    return jnp.concatenate([high, mid, low, high, mid, high], axis=axis)


def dot_nt(a, b):
    return lax.dot_general(a, b, (((1,), (1,)), ((), ())), preferred_element_type=F32)


def dot_nn(a, b):
    return lax.dot_general(a, b, (((1,), (0,)), ((), ())), preferred_element_type=F32)


def recip(x):
    return pltpu.reciprocal(x, approx=True)


def row_of(x, i):
    return jnp.broadcast_to(x[i : i + 1, :], (8, BK))


def col_of(x, j):
    return jnp.broadcast_to(x[:, j : j + 1], (8, BK))


def factor8(c):
    w = [[None] * 8 for _ in range(8)]
    rp = [None] * 8
    for i in range(8):
        w[i][i] = jnp.ones_like(c[0][0])
    for s in range(8):
        rp[s] = recip(c[s][s])
        for i in range(s + 1, 8):
            f = c[i][s] * rp[s]
            for j in range(s + 1, i + 1):
                c[i][j] = c[i][j] - f * c[j][s]
            for q in range(s):
                w[i][q] = w[i][q] - f * w[s][q]
            w[i][s] = -f
    return w, rp


def factor_inverse(a):
    tiles = [a[8 * t : 8 * t + 8, :] for t in range(16)]
    lane = lax.broadcasted_iota(jnp.int32, (8, BK), 1)
    sub = lax.broadcasted_iota(jnp.int32, (8, BK), 0)
    out = []
    for t in range(16):
        x, b0 = tiles[t], 8 * t
        cols = [col_of(x, b0 + j) for j in range(8)]
        w, rp = factor8([[row_of(cols[j], i) for j in range(i + 1)] for i in range(8)])
        inside = (lane >= b0) & (lane < b0 + 8)
        xt = jnp.where(inside, (lane - b0 == sub).astype(F32), x)
        r = [row_of(xt, i) for i in range(8)]
        u = []
        for s in range(8):
            y = r[s]
            for j in range(s):
                y = y + w[s][j] * r[j]
            u.append(y)
        y, p = u[0], rp[0]
        for s in range(1, 8):
            y = jnp.where(sub == s, u[s], y)
            p = jnp.where(sub == s, rp[s], p)
        out.append(jnp.where(lane <= b0 + sub, y * lax.sqrt(p), 0.0))
        for i in range(t + 1, 16):
            e = [col_of(tiles[i], b0 + j) for j in range(8)]
            z = jnp.where(inside, 0.0, tiles[i])
            for s in range(8):
                f = e[s]
                for j in range(s):
                    f = f + w[s][j] * e[j]
                z = z - (f * rp[s]) * u[s]
            tiles[i] = z
    return jnp.concatenate(out, axis=0)


def block_at(k):
    return pl.ds(pl.multiple_of(k * BK, BK), BK)


def factor_steps(a_ref, g_ref, diag, left_ref, right_ref, invl_ref, invr_ref, emit):
    rows = lax.broadcasted_iota(jnp.int32, (PANEL, BK), 0)
    diag[...] = a_ref[:BK, :BK]
    invl_ref[...] = jnp.zeros_like(invl_ref)
    invr_ref[...] = jnp.zeros_like(invr_ref)

    def step(k, carry):
        here = block_at(k)
        before = block_at(jnp.maximum(k - 1, 0))
        after = block_at(jnp.minimum(k + 1, NB - 1))
        block = diag[...]
        s_k = dot_nn(invl_ref[...], stack_right(g_ref[before, :], axis=0))
        panel = dot_nt(stack_left(a_ref[:, before]), invr_ref[...])
        panel = jnp.where(rows >= k * BK, panel, 0.0)
        left_ref[...] = stack_left(panel)
        right_ref[...] = stack_right(panel)
        for j in range(NB // 2):
            cols = slice(2 * BK * j, 2 * BK * (j + 1))
            a_ref[:, cols] -= dot_nt(left_ref[...], right_ref[cols, :])
        g_ref[...] -= dot_nn(left_ref[...], stack_right(s_k, axis=0))
        inverse = factor_inverse(block)
        inv_r = stack_right(inverse)
        invl_ref[...] = stack_left(inverse)
        invr_ref[...] = inv_r
        low = dot_nt(stack_left(a_ref[after, here]), inv_r)
        diag[...] = a_ref[after, after] - dot_nt(stack_left(low), stack_right(low))
        emit(k - 1, s_k)
        return carry

    lax.fori_loop(0, NB, step, 0)
    last = slice(PANEL - BK, PANEL)
    emit(NB - 1, dot_nn(invl_ref[...], stack_right(g_ref[last, :], axis=0)))


def kernel(
    markers_ref, out_ref,
    own, panel, a_ref, dpart, drecv, dred, gsend, grecv, g_ref, solved, diag, left_ref, right_ref, invl_ref, invr_ref,
    local_sem, ag_send, ag_recv, dag_send, dag_recv, rs_send, rs_recv, dc_send, dc_recv,
    gs_send, gs_recv, os_send, os_recv,
):
    row = lax.axis_index("row")
    col = lax.axis_index("col")
    core = lax.rem(row, 2)
    z = lax.rem(row // 2, 8)
    hi = row // 16

    def row_id(h, zz, q):
        return h * 16 + zz * 2 + q

    sibling = row_id(hi, z, 1 - core)
    partner = row_id(1 - hi, z, core)
    up = row_id(hi, lax.rem(z + 1, 8), core)
    down = row_id(hi, lax.rem(z + 7, 8), core)
    row_peers = (sibling, partner, up, down)
    col_peers = [lax.rem(col + o, NB) for o in range(1, NB)]

    load_panel = pltpu.make_async_copy(
        markers_ref.at[pl.ds(0, PB), :], panel.at[pl.ds(pl.multiple_of(row * PB, PB), PB), :], local_sem.at[0]
    )
    load_panel.start()
    load_own = pltpu.make_async_copy(markers_ref, own, local_sem.at[1])
    load_own.start()

    barrier = pltpu.get_barrier_semaphore()
    for peer in row_peers:
        pl.semaphore_signal(barrier, inc=1, device_id=(peer, col), device_id_type=MESH)
    for peer in col_peers:
        pl.semaphore_signal(barrier, inc=1, device_id=(row, peer), device_id_type=MESH)
    pl.semaphore_wait(barrier, len(row_peers) + len(col_peers))

    def piece_id(h, zz):
        return h * 8 + zz

    def gather(buf, send, recv, between):
        def block(r):
            return buf.at[pl.ds(pl.multiple_of(r * PB, PB), PB), :]

        started = []

        def copy(r, target, index, go=True):
            c = pltpu.make_async_remote_copy(
                src_ref=block(r), dst_ref=block(r), send_sem=send.at[index], recv_sem=recv.at[index],
                device_id=(target, col), device_id_type=MESH,
            )
            if go:
                c.start()
                started.append(c)
            return c

        def index_of(stream, way, d):
            return (stream * 2 + way) * 4 + d - 1

        def source(stream, way, d):
            h = hi if stream == 0 else 1 - hi
            zz = lax.rem(z + (8 - d if way == 0 else d), 8)
            return row_id(h, zz, core)

        def forward(stream, way, d):
            copy(source(stream, way, d), up if way == 0 else down, index_of(stream, way, d + 1))

        reach = {(0, 0): 4, (0, 1): 3, (1, 0): 3, (1, 1): 4}
        sib = 16
        sib_done = []

        def to_sibling(r, index):
            copy(r, sibling, index)
            sib_done.append(copy(r + 1 - 2 * core, sibling, index, go=False))

        def from_sibling():
            for c in sib_done:
                c.wait_recv()
            sib_done.clear()

        copy(row, partner, 32)
        forward(0, 0, 0)
        forward(0, 1, 0)
        to_sibling(row, sib)
        copy(partner, partner, 32, go=False).wait_recv()
        forward(1, 0, 0)
        forward(1, 1, 0)
        to_sibling(partner, sib + 1)
        n = 2
        for d in range(1, 5):
            ways = [sw for sw in ((0, 0), (0, 1), (1, 0), (1, 1)) if d <= reach[sw]]
            arrived = []
            for stream, way in ways:
                r = source(stream, way, d)
                copy(r, sibling, index_of(stream, way, d), go=False).wait_recv()
                if d < reach[stream, way]:
                    forward(stream, way, d)
                arrived.append(r)
            from_sibling()
            for r in arrived:
                to_sibling(r, sib + n)
                n += 1
            between(d)
        from_sibling()
        return started

    def pieces(d):
        if d == 0:
            return [piece_id(hi, z), piece_id(1 - hi, z)]
        plus, minus = lax.rem(z + 8 - d, 8), lax.rem(z + d, 8)
        if d == 4:
            return [piece_id(hi, plus), piece_id(1 - hi, plus)]
        return [piece_id(hi, plus), piece_id(hi, minus), piece_id(1 - hi, plus), piece_id(1 - hi, minus)]

    first_tile = [0, 1, 3, 5, 7]
    gram_copies = []

    def gram_chunk(d):
        ids = pieces(d)
        tiles = len(ids) // 2
        t0 = first_tile[d]
        chosen = jnp.concatenate([panel[pl.ds(pl.multiple_of(p * 64, 64), 64), :] for p in ids], axis=0)
        sums = dot_nt(own[...], chosen)
        for dest in range(NB):
            slot = lax.rem(dest + NB - col, NB)
            for t in range(tiles):
                gsend[t0 + t, slot] = sums[dest * BK : (dest + 1) * BK, t * BK : (t + 1) * BK]
        for o in range(1, NB):
            c = pltpu.make_async_remote_copy(
                src_ref=gsend.at[pl.ds(t0, tiles), o], dst_ref=grecv.at[pl.ds(t0, tiles), o],
                send_sem=gs_send.at[d * NB + o], recv_sem=gs_recv.at[d * NB + o],
                device_id=(row, col_peers[o - 1]), device_id_type=MESH,
            )
            c.start()
            gram_copies.append(c)

    load_panel.wait()

    def while_gathering(d):
        if d == 1:
            load_own.wait()
        if d < 4:
            gram_chunk(d - 1)

    started = gather(panel, ag_send, ag_recv, while_gathering)

    mine = pl.ds(pl.multiple_of(row * PB, PB), PB)
    here = pl.ds(pl.multiple_of(col * BK, BK), BK)
    dpart[...] = dot_nt(panel[mine, :], panel[...])

    def reduce_copy(o, target):
        return pltpu.make_async_remote_copy(
            src_ref=dpart.at[:, pl.ds(pl.multiple_of(target * BK, BK), BK)], dst_ref=drecv.at[o],
            send_sem=rs_send.at[o], recv_sem=rs_recv.at[o], device_id=(row, target), device_id_type=MESH,
        )

    scatter = [reduce_copy(o, col_peers[o - 1]) for o in range(1, NB)]
    for c in scatter:
        c.start()
    gram_chunk(3)
    for c in scatter:
        c.wait_recv()
    total = dpart[:, here]
    for o in range(1, NB):
        total = total + drecv[o]
    diagonal = (
        lax.broadcasted_iota(jnp.int32, (PB, BK), 0) + row * PB
        == lax.broadcasted_iota(jnp.int32, (PB, BK), 1) + col * BK
    )
    dred[...] = total * (1.0 / M) + jnp.where(diagonal, RIDGE, 0.0)
    a_ref[mine, here] = dred[...]

    def spread_copy(o, target):
        return pltpu.make_async_remote_copy(
            src_ref=dred, dst_ref=a_ref.at[mine, here],
            send_sem=dc_send.at[o], recv_sem=dc_recv.at[o], device_id=(row, target), device_id_type=MESH,
        )

    spread = [spread_copy(o, col_peers[o - 1]) for o in range(1, NB)]
    for c in spread:
        c.start()
    gram_chunk(4)
    for c in spread:
        c.wait_recv()

    def while_spreading(d):
        pass

    started += gather(a_ref, dag_send, dag_recv, while_spreading)

    for c in gram_copies:
        c.wait_recv()
    for d in range(5):
        ids = pieces(d)
        for t in range(len(ids) // 2):
            tile = first_tile[d] + t
            total = gsend[tile, 0]
            for s in range(1, NB):
                total = total + grecv[tile, s]
            total = jnp.transpose(total) * (1.0 / M)
            for half in range(2):
                g_ref[pl.ds(pl.multiple_of(ids[2 * t + half] * 64, 64), 64), :] = total[half * 64 : half * 64 + 64, :]
    ridge = (
        (lax.broadcasted_iota(jnp.int32, (PB, BK), 0) == lax.broadcasted_iota(jnp.int32, (PB, BK), 1))
        & (col == 0)
    )
    g_ref[mine, :] += jnp.where(ridge, RIDGE, 0.0)
    for c in started + scatter + spread + gram_copies:
        c.wait_send()

    def out_copy(k, source):
        return pltpu.make_async_remote_copy(
            src_ref=solved.at[block_at(k), :], dst_ref=out_ref.at[:, pl.ds(pl.multiple_of(source * BK, BK), BK)],
            send_sem=os_send.at[k], recv_sem=os_recv.at[source], device_id=(row, k), device_id_type=MESH,
        )

    def emit(k, rows):
        solved[block_at(jnp.maximum(k, 0)), :] = rows

        @pl.when((k >= 0) & (col != k))
        def _():
            out_copy(k, col).start()

    factor_steps(a_ref, g_ref, diag, left_ref, right_ref, invl_ref, invr_ref, emit)
    out_ref[:, here] = solved[here, :]
    for o in range(1, NB):
        k = col_peers[o - 1]
        out_copy(k, col).wait_send()
        out_copy(k, k).wait_recv()


def shards(markers):
    sem = pltpu.SemaphoreType.DMA
    return pl.pallas_call(
        kernel,
        out_shape=jax.ShapeDtypeStruct((BK, 1024), F32),
        in_specs=[pl.BlockSpec(memory_space=pl.ANY)],
        out_specs=pl.BlockSpec(memory_space=pltpu.VMEM),
        scratch_shapes=[
            pltpu.VMEM((1024, 2048), BF16),
            pltpu.VMEM((PANEL, 2048), BF16),
            pltpu.VMEM((PANEL, PANEL), F32),
            pltpu.VMEM((PB, PANEL), F32),
            pltpu.VMEM((NB, PB, BK), F32),
            pltpu.VMEM((PB, BK), F32),
            pltpu.VMEM((NB, NB, BK, BK), F32),
            pltpu.VMEM((NB, NB, BK, BK), F32),
            pltpu.VMEM((PANEL, BK), F32),
            pltpu.VMEM((PANEL, BK), F32),
            pltpu.VMEM((BK, BK), F32),
            pltpu.VMEM((PANEL, 6 * BK), BF16),
            pltpu.VMEM((PANEL, 6 * BK), BF16),
            pltpu.VMEM((BK, 6 * BK), BF16),
            pltpu.VMEM((BK, 6 * BK), BF16),
            sem((2,)), sem((33,)), sem((33,)), sem((33,)), sem((33,)),
            sem((NB,)), sem((NB,)), sem((NB,)), sem((NB,)),
            sem((5 * NB,)), sem((5 * NB,)), sem((NB,)), sem((NB,)),
        ],
        compiler_params=pltpu.CompilerParams(
            collective_id=0, has_side_effects=True, vmem_limit_bytes=58 * 1024 * 1024
        ),
    )(markers)


def solution(mesh):
    return jax.shard_map(
        shards, mesh=mesh, in_specs=(P("row", "col"),), out_specs=P("col", "row"), check_vma=False
    )
```

```python
import functools

import jax
import jax.numpy as jnp
from jax import lax
from jax.experimental import pallas as pl
from jax.experimental.pallas import tpu as pltpu
from jax.sharding import PartitionSpec as P

M = 16384
PANEL = 1024
PB = 32
NB = 8
BK = 128
RIDGE = 0.001
PARTS = 1
KEPT = 5
MESH = pl.DeviceIdType.MESH
F32 = jnp.float32
BF16 = jnp.bfloat16


def split3(x):
    high = x.astype(BF16)
    rest = x - high.astype(F32)
    mid = rest.astype(BF16)
    low = (rest - mid.astype(F32)).astype(BF16)
    return high, mid, low


def stack_left(x, axis=1):
    high, mid, low = split3(x)
    return jnp.concatenate([high, high, high, mid, mid, low], axis=axis)


def stack_right(x, axis=1):
    high, mid, low = split3(x)
    return jnp.concatenate([high, mid, low, high, mid, high], axis=axis)


def dot_nt(a, b):
    return lax.dot_general(a, b, (((1,), (1,)), ((), ())), preferred_element_type=F32)


def dot_nn(a, b):
    return lax.dot_general(a, b, (((1,), (0,)), ((), ())), preferred_element_type=F32)


def recip(x):
    return pltpu.reciprocal(x, approx=True)


def row_of(x, i):
    return jnp.broadcast_to(x[i : i + 1, :], (8, BK))


def col_of(x, j):
    return jnp.broadcast_to(x[:, j : j + 1], (8, BK))


def factor8(c):
    w = [[None] * 8 for _ in range(8)]
    rp = [None] * 8
    for i in range(8):
        w[i][i] = jnp.ones_like(c[0][0])
    for s in range(8):
        rp[s] = recip(c[s][s])
        for i in range(s + 1, 8):
            f = c[i][s] * rp[s]
            for j in range(s + 1, i + 1):
                c[i][j] = c[i][j] - f * c[j][s]
            for q in range(s):
                w[i][q] = w[i][q] - f * w[s][q]
            w[i][s] = -f
    return w, rp


def factor_inverse(a):
    tiles = [a[8 * t : 8 * t + 8, :] for t in range(16)]
    lane = lax.broadcasted_iota(jnp.int32, (8, BK), 1)
    sub = lax.broadcasted_iota(jnp.int32, (8, BK), 0)
    out = []
    for t in range(16):
        x, b0 = tiles[t], 8 * t
        cols = [col_of(x, b0 + j) for j in range(8)]
        w, rp = factor8([[row_of(cols[j], i) for j in range(i + 1)] for i in range(8)])
        inside = (lane >= b0) & (lane < b0 + 8)
        xt = jnp.where(inside, (lane - b0 == sub).astype(F32), x)
        r = [row_of(xt, i) for i in range(8)]
        u = []
        for s in range(8):
            y = r[s]
            for j in range(s):
                y = y + w[s][j] * r[j]
            u.append(y)
        y, p = u[0], rp[0]
        for s in range(1, 8):
            y = jnp.where(sub == s, u[s], y)
            p = jnp.where(sub == s, rp[s], p)
        out.append(jnp.where(lane <= b0 + sub, y * lax.sqrt(p), 0.0))
        for i in range(t + 1, 16):
            e = [col_of(tiles[i], b0 + j) for j in range(8)]
            z = jnp.where(inside, 0.0, tiles[i])
            for s in range(8):
                f = e[s]
                for j in range(s):
                    f = f + w[s][j] * e[j]
                z = z - (f * rp[s]) * u[s]
            tiles[i] = z
    return jnp.concatenate(out, axis=0)


def block_at(k):
    return pl.ds(pl.multiple_of(k * BK, BK), BK)


def factor_steps(a_ref, g_ref, diag, left_ref, right_ref, invl_ref, invr_ref, at_first, emit):
    rows = lax.broadcasted_iota(jnp.int32, (PANEL, BK), 0)
    diag[...] = a_ref[:BK, :BK]
    invl_ref[...] = jnp.zeros_like(invl_ref)
    invr_ref[...] = jnp.zeros_like(invr_ref)

    def step(k, carry):
        here = block_at(k)
        before = block_at(jnp.maximum(k - 1, 0))
        after = block_at(jnp.minimum(k + 1, NB - 1))
        block = diag[...]

        @pl.when(k == 1)
        def _():
            at_first()

        s_k = dot_nn(invl_ref[...], stack_right(g_ref[before, :], axis=0))
        panel = dot_nt(stack_left(a_ref[:, before]), invr_ref[...])
        panel = jnp.where(rows >= k * BK, panel, 0.0)
        left_ref[...] = stack_left(panel)
        right_ref[...] = stack_right(panel)
        for j in range(NB // 2):
            cols = slice(2 * BK * j, 2 * BK * (j + 1))
            a_ref[:, cols] -= dot_nt(left_ref[...], right_ref[cols, :])
        g_ref[...] -= dot_nn(left_ref[...], stack_right(s_k, axis=0))
        inverse = factor_inverse(block)
        inv_r = stack_right(inverse)
        invl_ref[...] = stack_left(inverse)
        invr_ref[...] = inv_r
        low = dot_nt(stack_left(a_ref[after, here]), inv_r)
        diag[...] = a_ref[after, after] - dot_nt(stack_left(low), stack_right(low))
        emit(k - 1, s_k)
        return carry

    lax.fori_loop(0, NB, step, 0)
    last = slice(PANEL - BK, PANEL)
    emit(NB - 1, dot_nn(invl_ref[...], stack_right(g_ref[last, :], axis=0)))


def kernel(
    markers_ref, out_ref,
    own, panel, a_ref, turned, dpart, drecv, dred, gsend, grecv, relay, g_ref, solved, diag, left_ref, right_ref, invl_ref, invr_ref,
    local_sem, ag_send, ag_recv, dag_send, dag_recv, rs_send, rs_recv, dc_send, dc_recv,
    gs_send, gs_recv, os_send, os_recv,
):
    row = lax.axis_index("row")
    col = lax.axis_index("col")
    core = lax.rem(row, 2)
    z = lax.rem(row // 2, 8)
    hi = row // 16

    def row_id(h, zz, q):
        return h * 16 + zz * 2 + q

    sibling = row_id(hi, z, 1 - core)
    partner = row_id(1 - hi, z, core)
    up = row_id(hi, lax.rem(z + 1, 8), core)
    down = row_id(hi, lax.rem(z + 7, 8), core)
    row_peers = (sibling, partner, up, down)
    col_peers = [lax.rem(col + o, NB) for o in range(1, NB)]

    load_panel = pltpu.make_async_copy(
        markers_ref.at[pl.ds(0, PB), :], panel.at[pl.ds(pl.multiple_of(row * PB, PB), PB), :], local_sem.at[0]
    )
    load_panel.start()
    load_own = pltpu.make_async_copy(markers_ref, own, local_sem.at[1])
    load_own.start()

    barrier = pltpu.get_barrier_semaphore()
    for peer in row_peers:
        pl.semaphore_signal(barrier, inc=1, device_id=(peer, col), device_id_type=MESH)
    for peer in col_peers:
        pl.semaphore_signal(barrier, inc=1, device_id=(row, peer), device_id_type=MESH)
    pl.semaphore_wait(barrier, len(row_peers) + len(col_peers))

    def piece_id(h, zz):
        return h * 8 + zz

    def gather(buf, width, send, recv, between):
        size = PB // PARTS

        def rows_of(r, part):
            if part is None:
                return buf.at[pl.ds(pl.multiple_of(r * PB, PB), PB), pl.ds(0, width)]
            return buf.at[pl.ds(pl.multiple_of(r * PB + part * size, size), size), pl.ds(0, width)]

        started = []

        def copy(r, part, target, index, go=True):
            c = pltpu.make_async_remote_copy(
                src_ref=rows_of(r, part), dst_ref=rows_of(r, part), send_sem=send.at[index], recv_sem=recv.at[index],
                device_id=(target, col), device_id_type=MESH,
            )
            if go:
                c.start()
                started.append(c)
            return c

        def index_of(stream, way, d, part):
            return 16 + PARTS + ((stream * 2 + way) * 4 + d - 1) * PARTS + part

        def source(stream, way, d):
            h = hi if stream == 0 else 1 - hi
            zz = lax.rem(z + (8 - d if way == 0 else d), 8)
            return row_id(h, zz, core)

        def forward(stream, way, d, part):
            copy(source(stream, way, d), part, up if way == 0 else down, index_of(stream, way, d + 1, part))

        reach = {(0, 0): 4, (0, 1): 3, (1, 0): 3, (1, 1): 4}
        sib_done = []

        def to_sibling(r, index):
            copy(r, None, sibling, index)
            sib_done.append(copy(r + 1 - 2 * core, None, sibling, index, go=False))

        def from_sibling():
            for c in sib_done:
                c.wait_recv()
            sib_done.clear()

        for part in range(PARTS):
            copy(row, part, partner, 16 + part)
            forward(0, 0, 0, part)
            forward(0, 1, 0, part)
        to_sibling(row, 0)
        for part in range(PARTS):
            copy(partner, part, partner, 16 + part, go=False).wait_recv()
            forward(1, 0, 0, part)
            forward(1, 1, 0, part)
        to_sibling(partner, 1)
        n = 2
        for d in range(1, 5):
            ways = [sw for sw in ((0, 0), (0, 1), (1, 0), (1, 1)) if d <= reach[sw]]
            for part in range(PARTS):
                for stream, way in ways:
                    copy(source(stream, way, d), part, sibling, index_of(stream, way, d, part), go=False).wait_recv()
                    if d < reach[stream, way]:
                        forward(stream, way, d, part)
            from_sibling()
            for stream, way in ways:
                to_sibling(source(stream, way, d), n)
                n += 1
            between(d)
        from_sibling()
        return started

    def pieces(d):
        if d == 0:
            return [piece_id(hi, z), piece_id(1 - hi, z)]
        plus, minus = lax.rem(z + 8 - d, 8), lax.rem(z + d, 8)
        if d == 4:
            return [piece_id(hi, plus), piece_id(1 - hi, plus)]
        return [piece_id(hi, plus), piece_id(hi, minus), piece_id(1 - hi, plus), piece_id(1 - hi, minus)]

    first_tile = [0, 1, 3, 5, 7]
    gram_copies = []

    def col_at(dx, dy):
        return lax.rem(col // 2 + dx, 4) * 2 + lax.rem(col + dy, 2)

    direct = [(0, 1), (1, 1), (3, 0), (1, 0), (3, 1)]

    def sums_copy(d, slot, target, buf, index, sem):
        t0, tiles = first_tile[d], len(pieces(d)) // 2
        c = pltpu.make_async_remote_copy(
            src_ref=gsend.at[pl.ds(t0, tiles), slot], dst_ref=buf.at[pl.ds(t0, tiles), index],
            send_sem=gs_send.at[d * NB + sem], recv_sem=gs_recv.at[d * NB + sem],
            device_id=(row, target), device_id_type=MESH,
        )
        c.start()
        return c

    def direct_copy(d, index):
        dx, dy = direct[index]
        gram_copies.append(sums_copy(d, dx * 2 + dy, col_at(dx, dy), grecv, index, index))

    relays = {}

    def gram_chunk(d):
        ids = pieces(d)
        t0 = first_tile[d]
        chosen = jnp.concatenate([panel[pl.ds(pl.multiple_of(p * 64, 64), 64), :] for p in ids], axis=0)
        sums = dot_nt(own[...], chosen)
        for dest in range(NB):
            slot = lax.rem(dest // 2 + 4 - col // 2, 4) * 2 + lax.rem(dest % 2 + 2 - lax.rem(col, 2), 2)
            for t in range(len(ids) // 2):
                gsend[t0 + t, slot] = sums[dest * BK : (dest + 1) * BK, t * BK : (t + 1) * BK]

    def gram_send(d):
        relays[d] = [
            sums_copy(d, 4, col_at(1, 0), relay, 0, 5),
            sums_copy(d, 5, col_at(3, 0), relay, 1, 6),
        ]
        for index in range(3):
            direct_copy(d, index)

    def gram_relay(d):
        for c in relays[d]:
            c.wait_recv()
        for t in range(first_tile[d], first_tile[d] + len(pieces(d)) // 2):
            gsend[t, 2] += relay[t, 0]
            gsend[t, 7] += relay[t, 1]
        for index in (3, 4):
            direct_copy(d, index)

    a_ref[...] = jnp.zeros_like(a_ref)
    g_ref[...] = jnp.zeros_like(g_ref)
    load_panel.wait()

    def while_gathering(d):
        if d == 1:
            load_own.wait()
        if d < 4:
            gram_chunk(d - 1)
            gram_send(d - 1)
        if d > 1:
            gram_relay(d - 2)

    started = gather(panel, 2048, ag_send, ag_recv, while_gathering)

    mine = pl.ds(pl.multiple_of(row * PB, PB), PB)
    here = pl.ds(pl.multiple_of(col * BK, BK), BK)
    dpart[...] = dot_nt(panel[mine, :], panel[...])

    def reduce_copy(o, target):
        return pltpu.make_async_remote_copy(
            src_ref=dpart.at[:, pl.ds(pl.multiple_of(target * BK, BK), BK)], dst_ref=drecv.at[o],
            send_sem=rs_send.at[o], recv_sem=rs_recv.at[o], device_id=(row, target), device_id_type=MESH,
        )

    scatter = [reduce_copy(o, col_peers[o - 1]) for o in range(1, NB)]
    for c in scatter:
        c.start()
    gram_chunk(3)
    for c in scatter:
        c.wait_recv()
    total = dpart[:, here]
    for o in range(1, NB):
        total = total + drecv[o]
    diagonal = (
        lax.broadcasted_iota(jnp.int32, (PB, BK), 0) + row * PB
        == lax.broadcasted_iota(jnp.int32, (PB, BK), 1) + col * BK
    )
    dred[...] = total * (1.0 / M) + jnp.where(diagonal, RIDGE, 0.0)
    kept = block_at(lax.rem(col + NB + KEPT - 1 - row // 4, NB))
    turned[mine, kept] = dred[...]

    def spread_copy(o, target):
        return pltpu.make_async_remote_copy(
            src_ref=dred, dst_ref=turned.at[mine, kept],
            send_sem=dc_send.at[o], recv_sem=dc_recv.at[o], device_id=(row, target), device_id_type=MESH,
        )

    spread = [spread_copy(o, col_peers[o - 1]) for o in range(1, NB)]
    for c in spread:
        c.start()
    gram_chunk(4)
    for c in spread:
        c.wait_recv()

    def while_spreading(d):
        if d == 1:
            gram_send(3)
            gram_send(4)
        elif d == 3:
            gram_relay(3)
            gram_relay(4)

    started += gather(turned, KEPT * BK, dag_send, dag_recv, while_spreading)
    for i in range(NB):
        for j in range(i + 1):
            m = (j - i + KEPT - 1) % NB
            if m < KEPT:
                a_ref[i * BK : (i + 1) * BK, j * BK : (j + 1) * BK] = turned[i * BK : (i + 1) * BK, m * BK : (m + 1) * BK]
            else:
                m = (i - j + KEPT - 1) % NB
                a_ref[i * BK : (i + 1) * BK, j * BK : (j + 1) * BK] = jnp.transpose(
                    turned[j * BK : (j + 1) * BK, m * BK : (m + 1) * BK]
                )

    def sum_gram():
        for c in gram_copies:
            c.wait_recv()
        for d in range(5):
            ids = pieces(d)
            for t in range(len(ids) // 2):
                tile = first_tile[d] + t
                total = gsend[tile, 0]
                for s in range(len(direct)):
                    total = total + grecv[tile, s]
                total = jnp.transpose(total) * (1.0 / M)
                for half in range(2):
                    rows = pl.ds(pl.multiple_of(ids[2 * t + half] * 64, 64), 64)
                    g_ref[rows, :] = total[half * 64 : half * 64 + 64, :]
        ridge = (
            (lax.broadcasted_iota(jnp.int32, (PB, BK), 0) == lax.broadcasted_iota(jnp.int32, (PB, BK), 1))
            & (col == 0)
        )
        g_ref[mine, :] += jnp.where(ridge, RIDGE, 0.0)

    def out_copy(k, source):
        return pltpu.make_async_remote_copy(
            src_ref=solved.at[block_at(k), :], dst_ref=out_ref.at[:, pl.ds(pl.multiple_of(source * BK, BK), BK)],
            send_sem=os_send.at[k], recv_sem=os_recv.at[source], device_id=(row, k), device_id_type=MESH,
        )

    def emit(k, rows):
        solved[block_at(jnp.maximum(k, 0)), :] = rows

        @pl.when((k >= 0) & (col != k))
        def _():
            out_copy(k, col).start()

    factor_steps(a_ref, g_ref, diag, left_ref, right_ref, invl_ref, invr_ref, sum_gram, emit)
    for c in started + scatter + spread + gram_copies:
        c.wait_send()
    for pair in relays.values():
        for c in pair:
            c.wait_send()
    out_ref[:, here] = solved[here, :]
    for o in range(1, NB):
        k = col_peers[o - 1]
        out_copy(k, col).wait_send()
        out_copy(k, k).wait_recv()


def shards(markers):
    sem = pltpu.SemaphoreType.DMA
    return pl.pallas_call(
        kernel,
        out_shape=jax.ShapeDtypeStruct((BK, 1024), F32),
        in_specs=[pl.BlockSpec(memory_space=pl.ANY)],
        out_specs=pl.BlockSpec(memory_space=pltpu.VMEM),
        scratch_shapes=[
            pltpu.VMEM((1024, 2048), BF16),
            pltpu.VMEM((PANEL, 2048), BF16),
            pltpu.VMEM((PANEL, PANEL), F32),
            pltpu.VMEM((PANEL, PANEL), F32),
            pltpu.VMEM((PB, PANEL), F32),
            pltpu.VMEM((NB, PB, BK), F32),
            pltpu.VMEM((PB, BK), F32),
            pltpu.VMEM((NB, NB, BK, BK), F32),
            pltpu.VMEM((NB, 5, BK, BK), F32),
            pltpu.VMEM((NB, 2, BK, BK), F32),
            pltpu.VMEM((PANEL, BK), F32),
            pltpu.VMEM((PANEL, BK), F32),
            pltpu.VMEM((BK, BK), F32),
            pltpu.VMEM((PANEL, 6 * BK), BF16),
            pltpu.VMEM((PANEL, 6 * BK), BF16),
            pltpu.VMEM((BK, 6 * BK), BF16),
            pltpu.VMEM((BK, 6 * BK), BF16),
            sem((2,)), sem((16 + 17 * PARTS,)), sem((16 + 17 * PARTS,)), sem((16 + 17 * PARTS,)), sem((16 + 17 * PARTS,)),
            sem((NB,)), sem((NB,)), sem((NB,)), sem((NB,)),
            sem((5 * NB,)), sem((5 * NB,)), sem((NB,)), sem((NB,)),
        ],
        compiler_params=pltpu.CompilerParams(
            collective_id=0, has_side_effects=True, vmem_limit_bytes=58 * 1024 * 1024
        ),
    )(markers)


def solution(mesh):
    return jax.shard_map(
        shards, mesh=mesh, in_specs=(P("row", "col"),), out_specs=P("col", "row"), check_vma=False
    )
```

```python
import functools

import jax
import jax.numpy as jnp
from jax import lax
from jax.experimental import pallas as pl
from jax.experimental.pallas import tpu as pltpu
from jax.sharding import PartitionSpec as P

M = 16384
PANEL = 1024
PB = 32
NB = 8
BK = 128
RIDGE = 0.001
PARTS = 1
KEPT = 5
MESH = pl.DeviceIdType.MESH
F32 = jnp.float32
BF16 = jnp.bfloat16


def split3(x):
    high = x.astype(BF16)
    rest = x - high.astype(F32)
    mid = rest.astype(BF16)
    low = (rest - mid.astype(F32)).astype(BF16)
    return high, mid, low


def stack_left(x, axis=1):
    high, mid, low = split3(x)
    return jnp.concatenate([high, high, high, mid, mid, low], axis=axis)


def stack_right(x, axis=1):
    high, mid, low = split3(x)
    return jnp.concatenate([high, mid, low, high, mid, high], axis=axis)


def dot_nt(a, b):
    return lax.dot_general(a, b, (((1,), (1,)), ((), ())), preferred_element_type=F32)


def dot_nn(a, b):
    return lax.dot_general(a, b, (((1,), (0,)), ((), ())), preferred_element_type=F32)


def recip(x):
    return pltpu.reciprocal(x, approx=True)


def row_of(x, i):
    return jnp.broadcast_to(x[i : i + 1, :], (8, BK))


def col_of(x, j):
    return jnp.broadcast_to(x[:, j : j + 1], (8, BK))


def factor8(c):
    w = [[None] * 8 for _ in range(8)]
    rp = [None] * 8
    for i in range(8):
        w[i][i] = jnp.ones_like(c[0][0])
    for s in range(8):
        rp[s] = recip(c[s][s])
        for i in range(s + 1, 8):
            f = c[i][s] * rp[s]
            for j in range(s + 1, i + 1):
                c[i][j] = c[i][j] - f * c[j][s]
            for q in range(s):
                w[i][q] = w[i][q] - f * w[s][q]
            w[i][s] = -f
    return w, rp


def factor_inverse(a):
    tiles = [a[8 * t : 8 * t + 8, :] for t in range(16)]
    lane = lax.broadcasted_iota(jnp.int32, (8, BK), 1)
    sub = lax.broadcasted_iota(jnp.int32, (8, BK), 0)
    out = []
    cols = [col_of(tiles[0], j) for j in range(8)]
    for t in range(16):
        x, b0 = tiles[t], 8 * t
        w, rp = factor8([[row_of(cols[j], i) for j in range(i + 1)] for i in range(8)])
        inside = (lane >= b0) & (lane < b0 + 8)

        def multipliers(i):
            e = [col_of(tiles[i], b0 + j) for j in range(8)]
            g = []
            for s in range(8):
                f = e[s]
                for j in range(s):
                    f = f + w[s][j] * e[j]
                g.append(f)
            return g

        if t < 15:
            g = multipliers(t + 1)
            f = [g[s] * rp[s] for s in range(8)]
            cols = [col_of(tiles[t + 1], b0 + 8 + j) for j in range(8)]
            for s in range(8):
                cols = [cols[j] - f[s] * row_of(g[s], j) for j in range(8)]
        xt = jnp.where(inside, (lane - b0 == sub).astype(F32), x)
        r = [row_of(xt, i) for i in range(8)]
        u = []
        for s in range(8):
            y = r[s]
            for j in range(s):
                y = y + w[s][j] * r[j]
            u.append(y)
        y, p = u[0], rp[0]
        for s in range(1, 8):
            y = jnp.where(sub == s, u[s], y)
            p = jnp.where(sub == s, rp[s], p)
        out.append(jnp.where(lane <= b0 + sub, y * lax.sqrt(p), 0.0))
        for i in range(t + 1, 16):
            if i > t + 1:
                f = [h * q for h, q in zip(multipliers(i), rp)]
            z = jnp.where(inside, 0.0, tiles[i])
            for s in range(8):
                z = z - f[s] * u[s]
            tiles[i] = z
    return jnp.concatenate(out, axis=0)


def block_at(k):
    return pl.ds(pl.multiple_of(k * BK, BK), BK)


def factor_steps(a_ref, g_ref, diag, left_ref, right_ref, invl_ref, invr_ref, at_first, emit):
    diag[...] = a_ref[:BK, :BK]
    invl_ref[...] = jnp.zeros_like(invl_ref)
    invr_ref[...] = jnp.zeros_like(invr_ref)

    def step(base, k, carry):
        here = block_at(k)
        before = block_at(jnp.maximum(k - 1, 0))
        after = block_at(jnp.minimum(k + 1, NB - 1))
        block = diag[...]

        if base == 0:
            @pl.when(k == 1)
            def _():
                at_first()

        s_k = dot_nn(invl_ref[...], stack_right(g_ref[before, :], axis=0))
        panel = dot_nt(stack_left(a_ref[base:, before]), invr_ref[...])
        rows = lax.broadcasted_iota(jnp.int32, (PANEL - base, BK), 0) + base
        panel = jnp.where(rows >= k * BK, panel, 0.0)
        left_ref[base:, :] = stack_left(panel)
        right_ref[base:, :] = stack_right(panel)
        for j in range(base // (2 * BK), NB // 2):
            cols = slice(2 * BK * j, 2 * BK * (j + 1))
            top = 0 if j < NB // 4 else PANEL // 2
            a_ref[top:, cols] -= dot_nt(left_ref[top:, :], right_ref[cols, :])
        g_ref[base:, :] -= dot_nn(left_ref[base:, :], stack_right(s_k, axis=0))
        inverse = factor_inverse(block)
        inv_r = stack_right(inverse)
        invl_ref[...] = stack_left(inverse)
        invr_ref[...] = inv_r
        low = dot_nt(stack_left(a_ref[after, here]), inv_r)
        diag[...] = a_ref[after, after] - dot_nt(stack_left(low), stack_right(low))
        emit(k - 1, s_k)
        return carry

    lax.fori_loop(0, NB // 2, functools.partial(step, 0), 0)
    lax.fori_loop(NB // 2, NB, functools.partial(step, PANEL // 2), 0)
    last = slice(PANEL - BK, PANEL)
    emit(NB - 1, dot_nn(invl_ref[...], stack_right(g_ref[last, :], axis=0)))


def kernel(
    markers_ref, out_ref,
    own, panel, a_ref, turned, dpart, drecv, dred, gsend, grecv, relay, g_ref, solved, diag, left_ref, right_ref, invl_ref, invr_ref,
    local_sem, ag_send, ag_recv, dag_send, dag_recv, rs_send, rs_recv, dc_send, dc_recv,
    gs_send, gs_recv, os_send, os_recv,
):
    row = lax.axis_index("row")
    col = lax.axis_index("col")
    core = lax.rem(row, 2)
    z = lax.rem(row // 2, 8)
    hi = row // 16

    def row_id(h, zz, q):
        return h * 16 + zz * 2 + q

    sibling = row_id(hi, z, 1 - core)
    partner = row_id(1 - hi, z, core)
    up = row_id(hi, lax.rem(z + 1, 8), core)
    down = row_id(hi, lax.rem(z + 7, 8), core)
    up2 = row_id(hi, lax.rem(z + 2, 8), core)
    down2 = row_id(hi, lax.rem(z + 6, 8), core)
    row_peers = (sibling, partner, up, down, up2, down2)
    col_peers = [lax.rem(col + o, NB) for o in range(1, NB)]

    load_panel = pltpu.make_async_copy(
        markers_ref.at[pl.ds(0, PB), :], panel.at[pl.ds(pl.multiple_of(row * PB, PB), PB), :], local_sem.at[0]
    )
    load_panel.start()
    load_own = pltpu.make_async_copy(markers_ref, own, local_sem.at[1])
    load_own.start()

    barrier = pltpu.get_barrier_semaphore()
    for peer in row_peers:
        pl.semaphore_signal(barrier, inc=1, device_id=(peer, col), device_id_type=MESH)
    for peer in col_peers:
        pl.semaphore_signal(barrier, inc=1, device_id=(row, peer), device_id_type=MESH)
    pl.semaphore_wait(barrier, len(row_peers) + len(col_peers))

    def piece_id(h, zz):
        return h * 8 + zz

    def gather(buf, width, skip, send, recv, between):
        size = PB // PARTS

        def rows_of(r, part):
            if part is None:
                return buf.at[pl.ds(pl.multiple_of(r * PB, PB), PB), pl.ds(0, width)]
            return buf.at[pl.ds(pl.multiple_of(r * PB + part * size, size), size), pl.ds(0, width)]

        started = []

        def copy(r, part, target, index, go=True):
            c = pltpu.make_async_remote_copy(
                src_ref=rows_of(r, part), dst_ref=rows_of(r, part), send_sem=send.at[index], recv_sem=recv.at[index],
                device_id=(target, col), device_id_type=MESH,
            )
            if go:
                c.start()
                started.append(c)
            return c

        def index_of(stream, way, d, part):
            return 16 + PARTS + ((stream * 2 + way) * 4 + d - 1) * PARTS + part

        def source(stream, way, d):
            h = hi if stream == 0 else 1 - hi
            zz = lax.rem(z + (8 - d if way == 0 else d), 8)
            return row_id(h, zz, core)

        def forward(stream, way, d, part):
            copy(source(stream, way, d), part, up if way == 0 else down, index_of(stream, way, d + 1, part))

        reach = {(0, 0): 4, (0, 1): 3, (1, 0): 3, (1, 1): 4}
        sib_done = []

        def to_sibling(r, index):
            copy(r, None, sibling, index)
            sib_done.append(copy(r + 1 - 2 * core, None, sibling, index, go=False))

        def from_sibling():
            for c in sib_done:
                c.wait_recv()
            sib_done.clear()

        for part in range(PARTS):
            copy(row, part, partner, 16 + part)
            forward(0, 0, 0, part)
            forward(0, 1, 0, part)
        to_sibling(row, 0)
        for part in range(PARTS):
            copy(partner, part, partner, 16 + part, go=False).wait_recv()
            forward(1, 0, 0, part)
            forward(1, 1, 0, part)
        to_sibling(partner, 1)
        n = 2
        for d in range(1, 5):
            ways = [sw for sw in ((0, 0), (0, 1), (1, 0), (1, 1)) if d <= reach[sw]]
            for part in range(PARTS):
                for stream, way in ways:
                    copy(source(stream, way, d), part, sibling, index_of(stream, way, d, part), go=False).wait_recv()
                    if d < (min(3, reach[stream, way]) if skip else reach[stream, way]):
                        forward(stream, way, d, part)
                    if skip and d == 2 and reach[stream, way] == 4:
                        far = up2 if way == 0 else down2
                        copy(source(stream, way, d), part, far, index_of(stream, way, 4, part))
            from_sibling()
            for stream, way in ways:
                to_sibling(source(stream, way, d), n)
                n += 1
            between(d)
        from_sibling()
        return started

    def pieces(d):
        if d == 0:
            return [piece_id(hi, z), piece_id(1 - hi, z)]
        plus, minus = lax.rem(z + 8 - d, 8), lax.rem(z + d, 8)
        if d == 4:
            return [piece_id(hi, plus), piece_id(1 - hi, plus)]
        return [piece_id(hi, plus), piece_id(hi, minus), piece_id(1 - hi, plus), piece_id(1 - hi, minus)]

    first_tile = [0, 1, 3, 5, 7]
    gram_copies = []

    def col_at(dx, dy):
        return lax.rem(col // 2 + dx, 4) * 2 + lax.rem(col + dy, 2)

    direct = [(0, 1), (1, 1), (3, 0), (1, 0), (3, 1)]

    def sums_copy(d, slot, target, buf, index, sem):
        t0, tiles = first_tile[d], len(pieces(d)) // 2
        c = pltpu.make_async_remote_copy(
            src_ref=gsend.at[pl.ds(t0, tiles), slot], dst_ref=buf.at[pl.ds(t0, tiles), index],
            send_sem=gs_send.at[d * NB + sem], recv_sem=gs_recv.at[d * NB + sem],
            device_id=(row, target), device_id_type=MESH,
        )
        c.start()
        return c

    def direct_copy(d, index):
        dx, dy = direct[index]
        gram_copies.append(sums_copy(d, dx * 2 + dy, col_at(dx, dy), grecv, index, index))

    relays = {}

    def gram_chunk(d):
        ids = pieces(d)
        t0 = first_tile[d]
        chosen = jnp.concatenate([panel[pl.ds(pl.multiple_of(p * 64, 64), 64), :] for p in ids], axis=0)
        sums = dot_nt(own[...], chosen)
        for dest in range(NB):
            slot = lax.rem(dest // 2 + 4 - col // 2, 4) * 2 + lax.rem(dest % 2 + 2 - lax.rem(col, 2), 2)
            for t in range(len(ids) // 2):
                gsend[t0 + t, slot] = sums[dest * BK : (dest + 1) * BK, t * BK : (t + 1) * BK]

    def gram_send(d):
        relays[d] = [
            sums_copy(d, 4, col_at(1, 0), relay, 0, 5),
            sums_copy(d, 5, col_at(3, 0), relay, 1, 6),
        ]
        for index in range(3):
            direct_copy(d, index)

    def gram_relay(d):
        for c in relays[d]:
            c.wait_recv()
        for t in range(first_tile[d], first_tile[d] + len(pieces(d)) // 2):
            gsend[t, 2] += relay[t, 0]
            gsend[t, 7] += relay[t, 1]
        for index in (3, 4):
            direct_copy(d, index)

    load_panel.wait()

    def while_gathering(d):
        if d == 1:
            load_own.wait()
            a_ref[...] = jnp.zeros_like(a_ref)
            g_ref[...] = jnp.zeros_like(g_ref)
        if d < 4:
            gram_chunk(d - 1)
            gram_send(d - 1)
        if d > 1:
            gram_relay(d - 2)

    started = gather(panel, 2048, False, ag_send, ag_recv, while_gathering)

    mine = pl.ds(pl.multiple_of(row * PB, PB), PB)
    here = pl.ds(pl.multiple_of(col * BK, BK), BK)
    dpart[...] = dot_nt(panel[mine, :], panel[...])

    def reduce_copy(o, target):
        return pltpu.make_async_remote_copy(
            src_ref=dpart.at[:, pl.ds(pl.multiple_of(target * BK, BK), BK)], dst_ref=drecv.at[o],
            send_sem=rs_send.at[o], recv_sem=rs_recv.at[o], device_id=(row, target), device_id_type=MESH,
        )

    scatter = [reduce_copy(o, col_peers[o - 1]) for o in range(1, NB)]
    for c in scatter:
        c.start()
    gram_chunk(3)
    for c in scatter:
        c.wait_recv()
    total = dpart[:, here]
    for o in range(1, NB):
        total = total + drecv[o]
    diagonal = (
        lax.broadcasted_iota(jnp.int32, (PB, BK), 0) + row * PB
        == lax.broadcasted_iota(jnp.int32, (PB, BK), 1) + col * BK
    )
    dred[...] = total * (1.0 / M) + jnp.where(diagonal, RIDGE, 0.0)
    kept = block_at(lax.rem(col + NB + KEPT - 1 - row // 4, NB))
    turned[mine, kept] = dred[...]

    def spread_copy(o, target):
        return pltpu.make_async_remote_copy(
            src_ref=dred, dst_ref=turned.at[mine, kept],
            send_sem=dc_send.at[o], recv_sem=dc_recv.at[o], device_id=(row, target), device_id_type=MESH,
        )

    spread = [spread_copy(o, col_peers[o - 1]) for o in range(1, NB)]
    for c in spread:
        c.start()
    gram_chunk(4)
    for c in spread:
        c.wait_recv()

    def while_spreading(d):
        if d == 1:
            gram_send(3)
            gram_send(4)
        elif d == 3:
            gram_relay(3)
            gram_relay(4)

    started += gather(turned, KEPT * BK, True, dag_send, dag_recv, while_spreading)
    for i in range(NB):
        for j in range(i + 1):
            m = (j - i + KEPT - 1) % NB
            if m < KEPT:
                a_ref[i * BK : (i + 1) * BK, j * BK : (j + 1) * BK] = turned[i * BK : (i + 1) * BK, m * BK : (m + 1) * BK]
            else:
                m = (i - j + KEPT - 1) % NB
                a_ref[i * BK : (i + 1) * BK, j * BK : (j + 1) * BK] = jnp.transpose(
                    turned[j * BK : (j + 1) * BK, m * BK : (m + 1) * BK]
                )

    def sum_gram():
        for c in gram_copies:
            c.wait_recv()
        for d in range(5):
            ids = pieces(d)
            for t in range(len(ids) // 2):
                tile = first_tile[d] + t
                total = gsend[tile, 0]
                for s in range(len(direct)):
                    total = total + grecv[tile, s]
                total = jnp.transpose(total) * (1.0 / M)
                for half in range(2):
                    rows = pl.ds(pl.multiple_of(ids[2 * t + half] * 64, 64), 64)
                    g_ref[rows, :] = total[half * 64 : half * 64 + 64, :]
        ridge = (
            (lax.broadcasted_iota(jnp.int32, (PB, BK), 0) == lax.broadcasted_iota(jnp.int32, (PB, BK), 1))
            & (col == 0)
        )
        g_ref[mine, :] += jnp.where(ridge, RIDGE, 0.0)

    def out_copy(k, source):
        return pltpu.make_async_remote_copy(
            src_ref=solved.at[block_at(k), :], dst_ref=out_ref.at[:, pl.ds(pl.multiple_of(source * BK, BK), BK)],
            send_sem=os_send.at[k], recv_sem=os_recv.at[source], device_id=(row, k), device_id_type=MESH,
        )

    def emit(k, rows):
        solved[block_at(jnp.maximum(k, 0)), :] = rows

        @pl.when((k >= 0) & (col != k))
        def _():
            out_copy(k, col).start()

    factor_steps(a_ref, g_ref, diag, left_ref, right_ref, invl_ref, invr_ref, sum_gram, emit)
    for c in started + scatter + spread + gram_copies:
        c.wait_send()
    for pair in relays.values():
        for c in pair:
            c.wait_send()
    out_ref[:, here] = solved[here, :]
    for o in range(1, NB):
        k = col_peers[o - 1]
        out_copy(k, col).wait_send()
        out_copy(k, k).wait_recv()


def shards(markers):
    sem = pltpu.SemaphoreType.DMA
    return pl.pallas_call(
        kernel,
        out_shape=jax.ShapeDtypeStruct((BK, 1024), F32),
        in_specs=[pl.BlockSpec(memory_space=pl.ANY)],
        out_specs=pl.BlockSpec(memory_space=pltpu.VMEM),
        scratch_shapes=[
            pltpu.VMEM((1024, 2048), BF16),
            pltpu.VMEM((PANEL, 2048), BF16),
            pltpu.VMEM((PANEL, PANEL), F32),
            pltpu.VMEM((PANEL, PANEL), F32),
            pltpu.VMEM((PB, PANEL), F32),
            pltpu.VMEM((NB, PB, BK), F32),
            pltpu.VMEM((PB, BK), F32),
            pltpu.VMEM((NB, NB, BK, BK), F32),
            pltpu.VMEM((NB, 5, BK, BK), F32),
            pltpu.VMEM((NB, 2, BK, BK), F32),
            pltpu.VMEM((PANEL, BK), F32),
            pltpu.VMEM((PANEL, BK), F32),
            pltpu.VMEM((BK, BK), F32),
            pltpu.VMEM((PANEL, 6 * BK), BF16),
            pltpu.VMEM((PANEL, 6 * BK), BF16),
            pltpu.VMEM((BK, 6 * BK), BF16),
            pltpu.VMEM((BK, 6 * BK), BF16),
            sem((2,)), sem((16 + 17 * PARTS,)), sem((16 + 17 * PARTS,)), sem((16 + 17 * PARTS,)), sem((16 + 17 * PARTS,)),
            sem((NB,)), sem((NB,)), sem((NB,)), sem((NB,)),
            sem((5 * NB,)), sem((5 * NB,)), sem((NB,)), sem((NB,)),
        ],
        compiler_params=pltpu.CompilerParams(
            collective_id=0, has_side_effects=True, vmem_limit_bytes=58 * 1024 * 1024
        ),
    )(markers)


def solution(mesh):
    return jax.shard_map(
        shards, mesh=mesh, in_specs=(P("row", "col"),), out_specs=P("col", "row"), check_vma=False
    )
```

```python
import functools

import jax
import jax.numpy as jnp
from jax import lax
from jax.experimental import pallas as pl
from jax.experimental.pallas import tpu as pltpu
from jax.sharding import PartitionSpec as P

M = 16384
PANEL = 1024
PB = 32
NB = 8
BK = 128
RIDGE = 0.001
PARTS = 1
KEPT = 5
MESH = pl.DeviceIdType.MESH
F32 = jnp.float32
BF16 = jnp.bfloat16


def split3(x):
    high = x.astype(BF16)
    rest = x - high.astype(F32)
    mid = rest.astype(BF16)
    low = (rest - mid.astype(F32)).astype(BF16)
    return high, mid, low


def stack_left(x, axis=1):
    high, mid, low = split3(x)
    return jnp.concatenate([high, high, high, mid, mid, low], axis=axis)


def stack_right(x, axis=1):
    high, mid, low = split3(x)
    return jnp.concatenate([high, mid, low, high, mid, high], axis=axis)


def dot_nt(a, b):
    return lax.dot_general(a, b, (((1,), (1,)), ((), ())), preferred_element_type=F32)


def dot_nn(a, b):
    return lax.dot_general(a, b, (((1,), (0,)), ((), ())), preferred_element_type=F32)


def recip(x):
    return pltpu.reciprocal(x, approx=True)


def row_of(x, i):
    return jnp.broadcast_to(x[i : i + 1, :], (8, BK))


def col_of(x, j):
    return jnp.broadcast_to(x[:, j : j + 1], (8, BK))


def factor8(c):
    w = [[None] * 8 for _ in range(8)]
    rp = [None] * 8
    for i in range(8):
        w[i][i] = jnp.ones_like(c[0][0])
    for s in range(8):
        rp[s] = recip(c[s][s])
        for i in range(s + 1, 8):
            f = c[i][s] * rp[s]
            for j in range(s + 1, i + 1):
                c[i][j] = c[i][j] - f * c[j][s]
            for q in range(s):
                w[i][q] = w[i][q] - f * w[s][q]
            w[i][s] = -f
    return w, rp


def factor_inverse(a):
    tiles = [a[8 * t : 8 * t + 8, :] for t in range(16)]
    lane = lax.broadcasted_iota(jnp.int32, (8, BK), 1)
    sub = lax.broadcasted_iota(jnp.int32, (8, BK), 0)
    out, scaled, plain = [], [], []
    cols = None
    for t in range(16):
        x, b0 = tiles[t], 8 * t
        end = 8 if t < 8 else 16
        if cols is None:
            cols = [col_of(x, b0 + j) for j in range(8)]
        w, rp = factor8([[row_of(cols[j], i) for j in range(i + 1)] for i in range(8)])
        inside = (lane >= b0) & (lane < b0 + 8)

        def multipliers(i):
            e = [col_of(tiles[i], b0 + j) for j in range(8)]
            g = []
            for s in range(8):
                f = e[s]
                for j in range(s):
                    f = f + w[s][j] * e[j]
                g.append(f)
            return g

        cols = None
        if t + 1 < end:
            g = multipliers(t + 1)
            f = [g[s] * rp[s] for s in range(8)]
            cols = [col_of(tiles[t + 1], b0 + 8 + j) for j in range(8)]
            for s in range(8):
                cols = [cols[j] - f[s] * row_of(g[s], j) for j in range(8)]
        xt = jnp.where(inside, (lane - b0 == sub).astype(F32), x)
        r = [row_of(xt, i) for i in range(8)]
        u = []
        for s in range(8):
            y = r[s]
            for j in range(s):
                y = y + w[s][j] * r[j]
            u.append(y)
        y, p = u[0], rp[0]
        for s in range(1, 8):
            y = jnp.where(sub == s, u[s], y)
            p = jnp.where(sub == s, rp[s], p)
        below = lane <= b0 + sub
        out.append(jnp.where(below, y * lax.sqrt(p), 0.0))
        for i in range(t + 1, end):
            if i > t + 1:
                f = [h * q for h, q in zip(multipliers(i), rp)]
            z = jnp.where(inside, 0.0, tiles[i])
            for s in range(8):
                z = z - f[s] * u[s]
            tiles[i] = z
        if t < 8:
            scaled.append(y * p)
            plain.append(jnp.where(below | (lane >= 64), y, 0.0))
        if t == 7:
            lh, lm, ll = (x.astype(F32) for x in split3(jnp.concatenate(scaled, axis=0)))
            rh, rm, rl = split3(jnp.concatenate(plain, axis=0))
            half = jnp.where(lax.broadcasted_iota(jnp.int32, (64, BK), 1) < 64, 0.0, jnp.concatenate(tiles[8:], axis=0))
            for left, right in (((lh, lm), (rl, rh)), ((lm, ll), (rm, rh)), ((lh, lh), (rh, rm))):
                turned = jnp.transpose(jnp.concatenate(left, axis=0))[64:, :].astype(BF16)
                half = half - dot_nn(turned, jnp.concatenate(right, axis=0))
            tiles[8:] = [half[8 * i : 8 * i + 8, :] for i in range(8)]
    return jnp.concatenate(out, axis=0)


def block_at(k):
    return pl.ds(pl.multiple_of(k * BK, BK), BK)


def factor_steps(a_ref, g_ref, diag, left_ref, right_ref, invl_ref, invr_ref, at_first, emit):
    diag[...] = a_ref[:BK, :BK]
    invl_ref[...] = jnp.zeros_like(invl_ref)
    invr_ref[...] = jnp.zeros_like(invr_ref)

    def step(base, k, carry):
        here = block_at(k)
        before = block_at(jnp.maximum(k - 1, 0))
        after = block_at(jnp.minimum(k + 1, NB - 1))
        block = diag[...]

        if base == 0:
            @pl.when(k == 1)
            def _():
                at_first()

        s_k = dot_nn(invl_ref[...], stack_right(g_ref[before, :], axis=0))
        panel = dot_nt(stack_left(a_ref[base:, before]), invr_ref[...])
        rows = lax.broadcasted_iota(jnp.int32, (PANEL - base, BK), 0) + base
        panel = jnp.where(rows >= k * BK, panel, 0.0)
        left_ref[base:, :] = stack_left(panel)
        right_ref[base:, :] = stack_right(panel)
        for j in range(base // (2 * BK), NB // 2):
            cols = slice(2 * BK * j, 2 * BK * (j + 1))
            top = 0 if j < NB // 4 else PANEL // 2
            a_ref[top:, cols] -= dot_nt(left_ref[top:, :], right_ref[cols, :])
        g_ref[base:, :] -= dot_nn(left_ref[base:, :], stack_right(s_k, axis=0))
        inverse = factor_inverse(block)
        inv_r = stack_right(inverse)
        invl_ref[...] = stack_left(inverse)
        invr_ref[...] = inv_r
        low = dot_nt(stack_left(a_ref[after, here]), inv_r)
        diag[...] = a_ref[after, after] - dot_nt(stack_left(low), stack_right(low))
        emit(k - 1, s_k)
        return carry

    lax.fori_loop(0, NB // 2, functools.partial(step, 0), 0)
    lax.fori_loop(NB // 2, NB, functools.partial(step, PANEL // 2), 0)
    last = slice(PANEL - BK, PANEL)
    emit(NB - 1, dot_nn(invl_ref[...], stack_right(g_ref[last, :], axis=0)))


def kernel(
    markers_ref, out_ref,
    own, panel, a_ref, turned, dpart, drecv, dred, gsend, grecv, relay, g_ref, solved, diag, left_ref, right_ref, invl_ref, invr_ref,
    local_sem, ag_send, ag_recv, dag_send, dag_recv, rs_send, rs_recv, dc_send, dc_recv,
    gs_send, gs_recv, os_send, os_recv,
):
    row = lax.axis_index("row")
    col = lax.axis_index("col")
    core = lax.rem(row, 2)
    z = lax.rem(row // 2, 8)
    hi = row // 16

    def row_id(h, zz, q):
        return h * 16 + zz * 2 + q

    sibling = row_id(hi, z, 1 - core)
    partner = row_id(1 - hi, z, core)
    up = row_id(hi, lax.rem(z + 1, 8), core)
    down = row_id(hi, lax.rem(z + 7, 8), core)
    up2 = row_id(hi, lax.rem(z + 2, 8), core)
    down2 = row_id(hi, lax.rem(z + 6, 8), core)
    row_peers = (sibling, partner, up, down, up2, down2)
    col_peers = [lax.rem(col + o, NB) for o in range(1, NB)]

    load_panel = pltpu.make_async_copy(
        markers_ref.at[pl.ds(0, PB), :], panel.at[pl.ds(pl.multiple_of(row * PB, PB), PB), :], local_sem.at[0]
    )
    load_panel.start()
    load_own = pltpu.make_async_copy(markers_ref, own, local_sem.at[1])
    load_own.start()

    barrier = pltpu.get_barrier_semaphore()
    for peer in row_peers:
        pl.semaphore_signal(barrier, inc=1, device_id=(peer, col), device_id_type=MESH)
    for peer in col_peers:
        pl.semaphore_signal(barrier, inc=1, device_id=(row, peer), device_id_type=MESH)
    pl.semaphore_wait(barrier, len(row_peers) + len(col_peers))

    def piece_id(h, zz):
        return h * 8 + zz

    def gather(buf, width, skip, send, recv, between):
        size = PB // PARTS

        def rows_of(r, part):
            if part is None:
                return buf.at[pl.ds(pl.multiple_of(r * PB, PB), PB), pl.ds(0, width)]
            return buf.at[pl.ds(pl.multiple_of(r * PB + part * size, size), size), pl.ds(0, width)]

        started = []

        def copy(r, part, target, index, go=True):
            c = pltpu.make_async_remote_copy(
                src_ref=rows_of(r, part), dst_ref=rows_of(r, part), send_sem=send.at[index], recv_sem=recv.at[index],
                device_id=(target, col), device_id_type=MESH,
            )
            if go:
                c.start()
                started.append(c)
            return c

        def index_of(stream, way, d, part):
            return 16 + PARTS + ((stream * 2 + way) * 4 + d - 1) * PARTS + part

        def source(stream, way, d):
            h = hi if stream == 0 else 1 - hi
            zz = lax.rem(z + (8 - d if way == 0 else d), 8)
            return row_id(h, zz, core)

        def forward(stream, way, d, part):
            copy(source(stream, way, d), part, up if way == 0 else down, index_of(stream, way, d + 1, part))

        reach = {(0, 0): 4, (0, 1): 3, (1, 0): 3, (1, 1): 4}
        sib_done = []

        def to_sibling(r, index):
            copy(r, None, sibling, index)
            sib_done.append(copy(r + 1 - 2 * core, None, sibling, index, go=False))

        def from_sibling():
            for c in sib_done:
                c.wait_recv()
            sib_done.clear()

        for part in range(PARTS):
            copy(row, part, partner, 16 + part)
            forward(0, 0, 0, part)
            forward(0, 1, 0, part)
        to_sibling(row, 0)
        for part in range(PARTS):
            copy(partner, part, partner, 16 + part, go=False).wait_recv()
            forward(1, 0, 0, part)
            forward(1, 1, 0, part)
        to_sibling(partner, 1)
        n = 2
        for d in range(1, 5):
            ways = [sw for sw in ((0, 0), (0, 1), (1, 0), (1, 1)) if d <= reach[sw]]
            for part in range(PARTS):
                for stream, way in ways:
                    copy(source(stream, way, d), part, sibling, index_of(stream, way, d, part), go=False).wait_recv()
                    if d < (min(3, reach[stream, way]) if skip else reach[stream, way]):
                        forward(stream, way, d, part)
                    if skip and d == 2 and reach[stream, way] == 4:
                        far = up2 if way == 0 else down2
                        copy(source(stream, way, d), part, far, index_of(stream, way, 4, part))
            from_sibling()
            for stream, way in ways:
                to_sibling(source(stream, way, d), n)
                n += 1
            between(d)
        from_sibling()
        return started

    def pieces(d):
        if d == 0:
            return [piece_id(hi, z), piece_id(1 - hi, z)]
        plus, minus = lax.rem(z + 8 - d, 8), lax.rem(z + d, 8)
        if d == 4:
            return [piece_id(hi, plus), piece_id(1 - hi, plus)]
        return [piece_id(hi, plus), piece_id(hi, minus), piece_id(1 - hi, plus), piece_id(1 - hi, minus)]

    first_tile = [0, 1, 3, 5, 7]
    gram_copies = []

    def col_at(dx, dy):
        return lax.rem(col // 2 + dx, 4) * 2 + lax.rem(col + dy, 2)

    direct = [(0, 1), (1, 1), (3, 0), (1, 0), (3, 1)]

    def sums_copy(d, slot, target, buf, index, sem):
        t0, tiles = first_tile[d], len(pieces(d)) // 2
        c = pltpu.make_async_remote_copy(
            src_ref=gsend.at[pl.ds(t0, tiles), slot], dst_ref=buf.at[pl.ds(t0, tiles), index],
            send_sem=gs_send.at[d * NB + sem], recv_sem=gs_recv.at[d * NB + sem],
            device_id=(row, target), device_id_type=MESH,
        )
        c.start()
        return c

    def direct_copy(d, index):
        dx, dy = direct[index]
        gram_copies.append(sums_copy(d, dx * 2 + dy, col_at(dx, dy), grecv, index, index))

    relays = {}

    def gram_chunk(d):
        ids = pieces(d)
        t0 = first_tile[d]
        chosen = jnp.concatenate([panel[pl.ds(pl.multiple_of(p * 64, 64), 64), :] for p in ids], axis=0)
        sums = dot_nt(own[...], chosen)
        for dest in range(NB):
            slot = lax.rem(dest // 2 + 4 - col // 2, 4) * 2 + lax.rem(dest % 2 + 2 - lax.rem(col, 2), 2)
            for t in range(len(ids) // 2):
                gsend[t0 + t, slot] = sums[dest * BK : (dest + 1) * BK, t * BK : (t + 1) * BK]

    def gram_send(d):
        relays[d] = [
            sums_copy(d, 4, col_at(1, 0), relay, 0, 5),
            sums_copy(d, 5, col_at(3, 0), relay, 1, 6),
        ]
        for index in range(3):
            direct_copy(d, index)

    def gram_relay(d):
        for c in relays[d]:
            c.wait_recv()
        for t in range(first_tile[d], first_tile[d] + len(pieces(d)) // 2):
            gsend[t, 2] += relay[t, 0]
            gsend[t, 7] += relay[t, 1]
        for index in (3, 4):
            direct_copy(d, index)

    load_panel.wait()

    def while_gathering(d):
        if d == 1:
            load_own.wait()
            a_ref[...] = jnp.zeros_like(a_ref)
            g_ref[...] = jnp.zeros_like(g_ref)
        if d < 4:
            gram_chunk(d - 1)
            gram_send(d - 1)
        if d in (2, 3):
            gram_relay(d - 2)

    started = gather(panel, 2048, False, ag_send, ag_recv, while_gathering)

    mine = pl.ds(pl.multiple_of(row * PB, PB), PB)
    here = pl.ds(pl.multiple_of(col * BK, BK), BK)
    dpart[...] = dot_nt(panel[mine, :], panel[...])

    def reduce_copy(o, target):
        return pltpu.make_async_remote_copy(
            src_ref=dpart.at[:, pl.ds(pl.multiple_of(target * BK, BK), BK)], dst_ref=drecv.at[o],
            send_sem=rs_send.at[o], recv_sem=rs_recv.at[o], device_id=(row, target), device_id_type=MESH,
        )

    scatter = [reduce_copy(o, col_peers[o - 1]) for o in range(1, NB)]
    for c in scatter:
        c.start()
    gram_chunk(3)
    for c in scatter:
        c.wait_recv()
    total = dpart[:, here]
    for o in range(1, NB):
        total = total + drecv[o]
    diagonal = (
        lax.broadcasted_iota(jnp.int32, (PB, BK), 0) + row * PB
        == lax.broadcasted_iota(jnp.int32, (PB, BK), 1) + col * BK
    )
    dred[...] = total * (1.0 / M) + jnp.where(diagonal, RIDGE, 0.0)
    kept = block_at(lax.rem(col + NB + KEPT - 1 - row // 4, NB))
    turned[mine, kept] = dred[...]

    def spread_copy(o, target):
        return pltpu.make_async_remote_copy(
            src_ref=dred, dst_ref=turned.at[mine, kept],
            send_sem=dc_send.at[o], recv_sem=dc_recv.at[o], device_id=(row, target), device_id_type=MESH,
        )

    spread = [spread_copy(o, col_peers[o - 1]) for o in range(1, NB)]
    for c in spread:
        c.start()
    gram_chunk(4)
    for c in spread:
        c.wait_recv()

    def while_spreading(d):
        if d == 1:
            gram_send(3)
            gram_send(4)
            gram_relay(2)
        elif d == 3:
            gram_relay(3)
            gram_relay(4)

    started += gather(turned, KEPT * BK, True, dag_send, dag_recv, while_spreading)
    for i in range(NB):
        for j in range(i + 1):
            m = (j - i + KEPT - 1) % NB
            if m < KEPT:
                a_ref[i * BK : (i + 1) * BK, j * BK : (j + 1) * BK] = turned[i * BK : (i + 1) * BK, m * BK : (m + 1) * BK]
            else:
                m = (i - j + KEPT - 1) % NB
                a_ref[i * BK : (i + 1) * BK, j * BK : (j + 1) * BK] = jnp.transpose(
                    turned[j * BK : (j + 1) * BK, m * BK : (m + 1) * BK]
                )

    def sum_gram():
        for c in gram_copies:
            c.wait_recv()
        for d in range(5):
            ids = pieces(d)
            for t in range(len(ids) // 2):
                tile = first_tile[d] + t
                total = gsend[tile, 0]
                for s in range(len(direct)):
                    total = total + grecv[tile, s]
                total = jnp.transpose(total) * (1.0 / M)
                for half in range(2):
                    rows = pl.ds(pl.multiple_of(ids[2 * t + half] * 64, 64), 64)
                    g_ref[rows, :] = total[half * 64 : half * 64 + 64, :]
        ridge = (
            (lax.broadcasted_iota(jnp.int32, (PB, BK), 0) == lax.broadcasted_iota(jnp.int32, (PB, BK), 1))
            & (col == 0)
        )
        g_ref[mine, :] += jnp.where(ridge, RIDGE, 0.0)

    def out_copy(k, source):
        return pltpu.make_async_remote_copy(
            src_ref=solved.at[block_at(k), :], dst_ref=out_ref.at[:, pl.ds(pl.multiple_of(source * BK, BK), BK)],
            send_sem=os_send.at[k], recv_sem=os_recv.at[source], device_id=(row, k), device_id_type=MESH,
        )

    def emit(k, rows):
        solved[block_at(jnp.maximum(k, 0)), :] = rows

        @pl.when((k >= 0) & (col != k))
        def _():
            out_copy(k, col).start()

    factor_steps(a_ref, g_ref, diag, left_ref, right_ref, invl_ref, invr_ref, sum_gram, emit)
    for c in started + scatter + spread + gram_copies:
        c.wait_send()
    for pair in relays.values():
        for c in pair:
            c.wait_send()
    out_ref[:, here] = solved[here, :]
    for o in range(1, NB):
        k = col_peers[o - 1]
        out_copy(k, col).wait_send()
        out_copy(k, k).wait_recv()


def shards(markers):
    sem = pltpu.SemaphoreType.DMA
    return pl.pallas_call(
        kernel,
        out_shape=jax.ShapeDtypeStruct((BK, 1024), F32),
        in_specs=[pl.BlockSpec(memory_space=pl.ANY)],
        out_specs=pl.BlockSpec(memory_space=pltpu.VMEM),
        scratch_shapes=[
            pltpu.VMEM((1024, 2048), BF16),
            pltpu.VMEM((PANEL, 2048), BF16),
            pltpu.VMEM((PANEL, PANEL), F32),
            pltpu.VMEM((PANEL, PANEL), F32),
            pltpu.VMEM((PB, PANEL), F32),
            pltpu.VMEM((NB, PB, BK), F32),
            pltpu.VMEM((PB, BK), F32),
            pltpu.VMEM((NB, NB, BK, BK), F32),
            pltpu.VMEM((NB, 5, BK, BK), F32),
            pltpu.VMEM((NB, 2, BK, BK), F32),
            pltpu.VMEM((PANEL, BK), F32),
            pltpu.VMEM((PANEL, BK), F32),
            pltpu.VMEM((BK, BK), F32),
            pltpu.VMEM((PANEL, 6 * BK), BF16),
            pltpu.VMEM((PANEL, 6 * BK), BF16),
            pltpu.VMEM((BK, 6 * BK), BF16),
            pltpu.VMEM((BK, 6 * BK), BF16),
            sem((2,)), sem((16 + 17 * PARTS,)), sem((16 + 17 * PARTS,)), sem((16 + 17 * PARTS,)), sem((16 + 17 * PARTS,)),
            sem((NB,)), sem((NB,)), sem((NB,)), sem((NB,)),
            sem((5 * NB,)), sem((5 * NB,)), sem((NB,)), sem((NB,)),
        ],
        compiler_params=pltpu.CompilerParams(
            collective_id=0, has_side_effects=True, vmem_limit_bytes=58 * 1024 * 1024
        ),
    )(markers)


def solution(mesh):
    return jax.shard_map(
        shards, mesh=mesh, in_specs=(P("row", "col"),), out_specs=P("col", "row"), check_vma=False
    )
```

```python
import functools

import jax
import jax.numpy as jnp
from jax import lax
from jax.experimental import pallas as pl
from jax.experimental.pallas import tpu as pltpu
from jax.sharding import PartitionSpec as P

M = 16384
PANEL = 1024
PB = 32
NB = 8
BK = 128
RIDGE = 0.001
PARTS = 1
KEPT = 5
MESH = pl.DeviceIdType.MESH
F32 = jnp.float32
BF16 = jnp.bfloat16


def split3(x):
    high = x.astype(BF16)
    rest = x - high.astype(F32)
    mid = rest.astype(BF16)
    low = (rest - mid.astype(F32)).astype(BF16)
    return high, mid, low


def stack_left(x, axis=1):
    high, mid, low = split3(x)
    return jnp.concatenate([high, high, high, mid, mid, low], axis=axis)


def stack_right(x, axis=1):
    high, mid, low = split3(x)
    return jnp.concatenate([high, mid, low, high, mid, high], axis=axis)


def dot_nt(a, b):
    return lax.dot_general(a, b, (((1,), (1,)), ((), ())), preferred_element_type=F32)


def dot_nn(a, b):
    return lax.dot_general(a, b, (((1,), (0,)), ((), ())), preferred_element_type=F32)


def recip(x):
    return pltpu.reciprocal(x, approx=True)


def row_of(x, i):
    return jnp.broadcast_to(x[i : i + 1, :], (8, BK))


def col_of(x, j):
    return jnp.broadcast_to(x[:, j : j + 1], (8, BK))


def factor8(c):
    w = [[None] * 8 for _ in range(8)]
    rp = [None] * 8
    for i in range(8):
        w[i][i] = jnp.ones_like(c[0][0])
    for s in range(8):
        rp[s] = recip(c[s][s])
        for i in range(s + 1, 8):
            f = c[i][s] * rp[s]
            for j in range(s + 1, i + 1):
                c[i][j] = c[i][j] - f * c[j][s]
            for q in range(s):
                w[i][q] = w[i][q] - f * w[s][q]
            w[i][s] = -f
    return w, rp


def factor_inverse(a):
    tiles = [a[8 * t : 8 * t + 8, :] for t in range(16)]
    lane = lax.broadcasted_iota(jnp.int32, (8, BK), 1)
    sub = lax.broadcasted_iota(jnp.int32, (8, BK), 0)
    out, scaled, plain = [], [], []
    cols = None
    for t in range(16):
        x, b0 = tiles[t], 8 * t
        end = 8 if t < 8 else 16
        if cols is None:
            cols = [col_of(x, b0 + j) for j in range(8)]
        w, rp = factor8([[row_of(cols[j], i) for j in range(i + 1)] for i in range(8)])
        inside = (lane >= b0) & (lane < b0 + 8)

        def multipliers(i):
            e = [col_of(tiles[i], b0 + j) for j in range(8)]
            g = []
            for s in range(8):
                f = e[s]
                for j in range(s):
                    f = f + w[s][j] * e[j]
                g.append(f)
            return g

        cols = None
        if t + 1 < end:
            g = multipliers(t + 1)
            f = [g[s] * rp[s] for s in range(8)]
            cols = [col_of(tiles[t + 1], b0 + 8 + j) for j in range(8)]
            for s in range(8):
                cols = [cols[j] - f[s] * row_of(g[s], j) for j in range(8)]
        xt = jnp.where(inside, (lane - b0 == sub).astype(F32), x)
        r = [row_of(xt, i) for i in range(8)]
        u = []
        for s in range(8):
            y = r[s]
            for j in range(s):
                y = y + w[s][j] * r[j]
            u.append(y)
        y, p = u[0], rp[0]
        for s in range(1, 8):
            y = jnp.where(sub == s, u[s], y)
            p = jnp.where(sub == s, rp[s], p)
        below = lane <= b0 + sub
        out.append(jnp.where(below, y * lax.sqrt(p), 0.0))
        for i in range(t + 1, end):
            if i > t + 1:
                f = [h * q for h, q in zip(multipliers(i), rp)]
            z = jnp.where(inside, 0.0, tiles[i])
            for s in range(8):
                z = z - f[s] * u[s]
            tiles[i] = z
        if t < 8:
            scaled.append(y * p)
            plain.append(jnp.where(below | (lane >= 64), y, 0.0))
        if t == 7:
            lh, lm, ll = (x.astype(F32) for x in split3(jnp.concatenate(scaled, axis=0)))
            rh, rm, rl = split3(jnp.concatenate(plain, axis=0))
            half = jnp.where(lax.broadcasted_iota(jnp.int32, (64, BK), 1) < 64, 0.0, jnp.concatenate(tiles[8:], axis=0))
            for left, right in (((lh, lm), (rl, rh)), ((lm, ll), (rm, rh)), ((lh, lh), (rh, rm))):
                turned = jnp.transpose(jnp.concatenate(left, axis=0))[64:, :].astype(BF16)
                half = half - dot_nn(turned, jnp.concatenate(right, axis=0))
            tiles[8:] = [half[8 * i : 8 * i + 8, :] for i in range(8)]
    return jnp.concatenate(out, axis=0)


def block_at(k):
    return pl.ds(pl.multiple_of(k * BK, BK), BK)


def factor_steps(a_ref, g_ref, diag, left_ref, right_ref, invl_ref, invr_ref, at_first, emit):
    diag[...] = a_ref[:BK, :BK]
    invl_ref[...] = jnp.zeros_like(invl_ref)
    invr_ref[...] = jnp.zeros_like(invr_ref)

    def step(base, k, carry):
        here = block_at(k)
        before = block_at(jnp.maximum(k - 1, 0))
        after = block_at(jnp.minimum(k + 1, NB - 1))
        block = diag[...]

        if base == 0:
            @pl.when(k == 1)
            def _():
                at_first()

        s_k = dot_nn(invl_ref[...], stack_right(g_ref[before, :], axis=0))
        panel = dot_nt(stack_left(a_ref[base:, before]), invr_ref[...])
        rows = lax.broadcasted_iota(jnp.int32, (PANEL - base, BK), 0) + base
        panel = jnp.where(rows >= k * BK, panel, 0.0)
        left_ref[base:, :] = stack_left(panel)
        right_ref[base:, :] = stack_right(panel)
        for j in range(base // (2 * BK), NB // 2):
            cols = slice(2 * BK * j, 2 * BK * (j + 1))
            top = 0 if j < NB // 4 else PANEL // 2
            a_ref[top:, cols] -= dot_nt(left_ref[top:, :], right_ref[cols, :])
        g_ref[base:, :] -= dot_nn(left_ref[base:, :], stack_right(s_k, axis=0))
        inverse = factor_inverse(block)
        inv_r = stack_right(inverse)
        invl_ref[...] = stack_left(inverse)
        invr_ref[...] = inv_r
        low = dot_nt(stack_left(a_ref[after, here]), inv_r)
        diag[...] = a_ref[after, after] - dot_nt(stack_left(low), stack_right(low))
        emit(k - 1, s_k)
        return carry

    lax.fori_loop(0, NB // 2, functools.partial(step, 0), 0)
    lax.fori_loop(NB // 2, NB, functools.partial(step, PANEL // 2), 0)
    last = slice(PANEL - BK, PANEL)
    emit(NB - 1, dot_nn(invl_ref[...], stack_right(g_ref[last, :], axis=0)))


def kernel(
    markers_ref, out_ref,
    own, panel, a_ref, turned, dpart, drecv, dred, gsend, grecv, relay, g_ref, solved, diag, left_ref, right_ref, invl_ref, invr_ref,
    local_sem, ag_send, ag_recv, dag_send, dag_recv, rs_send, rs_recv, dc_send, dc_recv,
    gs_send, gs_recv, os_send, os_recv,
):
    row = lax.axis_index("row")
    col = lax.axis_index("col")
    core = lax.rem(row, 2)
    z = lax.rem(row // 2, 8)
    hi = row // 16

    def row_id(h, zz, q):
        return h * 16 + zz * 2 + q

    sibling = row_id(hi, z, 1 - core)
    partner = row_id(1 - hi, z, core)
    up = row_id(hi, lax.rem(z + 1, 8), core)
    down = row_id(hi, lax.rem(z + 7, 8), core)
    up2 = row_id(hi, lax.rem(z + 2, 8), core)
    down2 = row_id(hi, lax.rem(z + 6, 8), core)
    row_peers = (sibling, partner, up, down, up2, down2)
    col_peers = [lax.rem(col + o, NB) for o in range(1, NB)]

    load_panel = pltpu.make_async_copy(
        markers_ref.at[pl.ds(0, PB), :], panel.at[pl.ds(pl.multiple_of(row * PB, PB), PB), :], local_sem.at[0]
    )
    load_panel.start()
    load_own = pltpu.make_async_copy(markers_ref, own, local_sem.at[1])
    load_own.start()

    barrier = pltpu.get_barrier_semaphore()
    for peer in row_peers:
        pl.semaphore_signal(barrier, inc=1, device_id=(peer, col), device_id_type=MESH)
    for peer in col_peers:
        pl.semaphore_signal(barrier, inc=1, device_id=(row, peer), device_id_type=MESH)
    pl.semaphore_wait(barrier, len(row_peers) + len(col_peers))

    def piece_id(h, zz):
        return h * 8 + zz

    def gather(buf, width, skip, send, recv, between):
        size = PB // PARTS

        def rows_of(r, part):
            if part is None:
                return buf.at[pl.ds(pl.multiple_of(r * PB, PB), PB), pl.ds(0, width)]
            return buf.at[pl.ds(pl.multiple_of(r * PB + part * size, size), size), pl.ds(0, width)]

        started = []

        def copy(r, part, target, index, go=True):
            c = pltpu.make_async_remote_copy(
                src_ref=rows_of(r, part), dst_ref=rows_of(r, part), send_sem=send.at[index], recv_sem=recv.at[index],
                device_id=(target, col), device_id_type=MESH,
            )
            if go:
                c.start()
                started.append(c)
            return c

        def index_of(stream, way, d, part):
            return 16 + PARTS + ((stream * 2 + way) * 4 + d - 1) * PARTS + part

        def source(stream, way, d):
            h = hi if stream == 0 else 1 - hi
            zz = lax.rem(z + (8 - d if way == 0 else d), 8)
            return row_id(h, zz, core)

        def forward(stream, way, d, part):
            copy(source(stream, way, d), part, up if way == 0 else down, index_of(stream, way, d + 1, part))

        reach = {(0, 0): 4, (0, 1): 3, (1, 0): 3, (1, 1): 4}
        sib_done = []

        def to_sibling(r, index):
            copy(r, None, sibling, index)
            sib_done.append(copy(r + 1 - 2 * core, None, sibling, index, go=False))

        def from_sibling():
            for c in sib_done:
                c.wait_recv()
            sib_done.clear()

        for part in range(PARTS):
            copy(row, part, partner, 16 + part)
            forward(0, 0, 0, part)
            forward(0, 1, 0, part)
        to_sibling(row, 0)
        for part in range(PARTS):
            copy(partner, part, partner, 16 + part, go=False).wait_recv()
            forward(1, 0, 0, part)
            forward(1, 1, 0, part)
        to_sibling(partner, 1)
        n = 2
        for d in range(1, 5):
            ways = [sw for sw in ((0, 0), (0, 1), (1, 0), (1, 1)) if d <= reach[sw]]
            for part in range(PARTS):
                for stream, way in ways:
                    copy(source(stream, way, d), part, sibling, index_of(stream, way, d, part), go=False).wait_recv()
                    if d < (min(3, reach[stream, way]) if skip else reach[stream, way]):
                        forward(stream, way, d, part)
                    if skip and d == 2 and reach[stream, way] == 4:
                        far = up2 if way == 0 else down2
                        copy(source(stream, way, d), part, far, index_of(stream, way, 4, part))
            from_sibling()
            for stream, way in ways:
                to_sibling(source(stream, way, d), n)
                n += 1
            between(d)
        from_sibling()
        return started

    def pieces(d):
        if d == 0:
            return [piece_id(hi, z), piece_id(1 - hi, z)]
        plus, minus = lax.rem(z + 8 - d, 8), lax.rem(z + d, 8)
        if d == 4:
            return [piece_id(hi, plus), piece_id(1 - hi, plus)]
        return [piece_id(hi, plus), piece_id(hi, minus), piece_id(1 - hi, plus), piece_id(1 - hi, minus)]

    first_tile = [0, 1, 3, 5, 7]
    gram_copies = [[] for _ in range(5)]

    def col_at(dx, dy):
        return lax.rem(col // 2 + dx, 4) * 2 + lax.rem(col + dy, 2)

    direct = [(0, 1), (1, 1), (3, 0), (1, 0), (3, 1)]

    def sums_copy(d, slot, target, buf, index, sem):
        t0, tiles = first_tile[d], len(pieces(d)) // 2
        c = pltpu.make_async_remote_copy(
            src_ref=gsend.at[pl.ds(t0, tiles), slot], dst_ref=buf.at[pl.ds(t0, tiles), index],
            send_sem=gs_send.at[d * NB + sem], recv_sem=gs_recv.at[d * NB + sem],
            device_id=(row, target), device_id_type=MESH,
        )
        c.start()
        return c

    def direct_copy(d, index):
        dx, dy = direct[index]
        gram_copies[d].append(sums_copy(d, dx * 2 + dy, col_at(dx, dy), grecv, index, index))

    relays = {}

    def gram_chunk(d):
        ids = pieces(d)
        t0 = first_tile[d]
        chosen = jnp.concatenate([panel[pl.ds(pl.multiple_of(p * 64, 64), 64), :] for p in ids], axis=0)
        sums = dot_nt(own[...], chosen)
        for dest in range(NB):
            slot = lax.rem(dest // 2 + 4 - col // 2, 4) * 2 + lax.rem(dest % 2 + 2 - lax.rem(col, 2), 2)
            for t in range(len(ids) // 2):
                gsend[t0 + t, slot] = sums[dest * BK : (dest + 1) * BK, t * BK : (t + 1) * BK]

    def gram_send(d):
        relays[d] = [
            sums_copy(d, 4, col_at(1, 0), relay, 0, 5),
            sums_copy(d, 5, col_at(3, 0), relay, 1, 6),
        ]
        for index in range(3):
            direct_copy(d, index)

    def gram_relay(d):
        for c in relays[d]:
            c.wait_recv()
        for t in range(first_tile[d], first_tile[d] + len(pieces(d)) // 2):
            gsend[t, 2] += relay[t, 0]
            gsend[t, 7] += relay[t, 1]
        for index in (3, 4):
            direct_copy(d, index)

    load_panel.wait()

    def while_gathering(d):
        if d == 1:
            load_own.wait()
            a_ref[...] = jnp.zeros_like(a_ref)
            g_ref[...] = jnp.zeros_like(g_ref)
        if d < 4:
            gram_chunk(d - 1)
            gram_send(d - 1)
        if d in (2, 3):
            gram_relay(d - 2)
        if d == 4:
            for o in (1, 2, 3):
                for h in range(2):
                    diagonal_part(h, o)

    mine = pl.ds(pl.multiple_of(row * PB, PB), PB)
    here = pl.ds(pl.multiple_of(col * BK, BK), BK)

    def diagonal_part(h, o):
        tile = h * 4 + lax.rem(lax.rem(z + 4, 8) // 2 + o, 4)
        cols = pl.ds(pl.multiple_of(tile * BK, BK), BK)
        dpart[:, cols] = dot_nt(panel[mine, :], panel[cols, :])

    started = gather(panel, 2048, False, ag_send, ag_recv, while_gathering)

    for h in range(2):
        diagonal_part(h, 0)

    def reduce_copy(o, target):
        return pltpu.make_async_remote_copy(
            src_ref=dpart.at[:, pl.ds(pl.multiple_of(target * BK, BK), BK)], dst_ref=drecv.at[o],
            send_sem=rs_send.at[o], recv_sem=rs_recv.at[o], device_id=(row, target), device_id_type=MESH,
        )

    scatter = [reduce_copy(o, col_peers[o - 1]) for o in range(1, NB)]
    for c in scatter:
        c.start()
    gram_chunk(3)
    for c in scatter:
        c.wait_recv()
    total = dpart[:, here]
    for o in range(1, NB):
        total = total + drecv[o]
    diagonal = (
        lax.broadcasted_iota(jnp.int32, (PB, BK), 0) + row * PB
        == lax.broadcasted_iota(jnp.int32, (PB, BK), 1) + col * BK
    )
    dred[...] = total * (1.0 / M) + jnp.where(diagonal, RIDGE, 0.0)
    kept = block_at(lax.rem(col + NB + KEPT - 1 - row // 4, NB))
    turned[mine, kept] = dred[...]

    def spread_copy(o, target):
        return pltpu.make_async_remote_copy(
            src_ref=dred, dst_ref=turned.at[mine, kept],
            send_sem=dc_send.at[o], recv_sem=dc_recv.at[o], device_id=(row, target), device_id_type=MESH,
        )

    spread = [spread_copy(o, col_peers[o - 1]) for o in range(1, NB)]
    for c in spread:
        c.start()
    gram_chunk(4)
    for c in spread:
        c.wait_recv()

    def sum_chunk(d):
        for c in gram_copies[d]:
            c.wait_recv()
        ids = pieces(d)
        for t in range(len(ids) // 2):
            tile = first_tile[d] + t
            total = gsend[tile, 0]
            for s in range(len(direct)):
                total = total + grecv[tile, s]
            total = jnp.transpose(total) * (1.0 / M)
            for half in range(2):
                rows = pl.ds(pl.multiple_of(ids[2 * t + half] * 64, 64), 64)
                g_ref[rows, :] = total[half * 64 : half * 64 + 64, :]

    def while_spreading(d):
        if d == 1:
            gram_send(3)
            gram_send(4)
            gram_relay(2)
        elif d == 3:
            gram_relay(3)
            gram_relay(4)
        elif d == 2:
            sum_chunk(0)
            sum_chunk(1)

    started += gather(turned, KEPT * BK, True, dag_send, dag_recv, while_spreading)
    for i in range(NB):
        for j in range(i + 1):
            m = (j - i + KEPT - 1) % NB
            if m < KEPT:
                a_ref[i * BK : (i + 1) * BK, j * BK : (j + 1) * BK] = turned[i * BK : (i + 1) * BK, m * BK : (m + 1) * BK]
            else:
                m = (i - j + KEPT - 1) % NB
                a_ref[i * BK : (i + 1) * BK, j * BK : (j + 1) * BK] = jnp.transpose(
                    turned[j * BK : (j + 1) * BK, m * BK : (m + 1) * BK]
                )

    def sum_gram():
        for d in (2, 3, 4):
            sum_chunk(d)
        ridge = (
            (lax.broadcasted_iota(jnp.int32, (PB, BK), 0) == lax.broadcasted_iota(jnp.int32, (PB, BK), 1))
            & (col == 0)
        )
        g_ref[mine, :] += jnp.where(ridge, RIDGE, 0.0)

    def out_copy(k, source):
        return pltpu.make_async_remote_copy(
            src_ref=solved.at[block_at(k), :], dst_ref=out_ref.at[:, pl.ds(pl.multiple_of(source * BK, BK), BK)],
            send_sem=os_send.at[k], recv_sem=os_recv.at[source], device_id=(row, k), device_id_type=MESH,
        )

    def emit(k, rows):
        solved[block_at(jnp.maximum(k, 0)), :] = rows

        @pl.when((k >= 0) & (col != k))
        def _():
            out_copy(k, col).start()

    factor_steps(a_ref, g_ref, diag, left_ref, right_ref, invl_ref, invr_ref, sum_gram, emit)
    for c in started + scatter + spread + sum(gram_copies, []):
        c.wait_send()
    for pair in relays.values():
        for c in pair:
            c.wait_send()
    out_ref[:, here] = solved[here, :]
    for o in range(1, NB):
        k = col_peers[o - 1]
        out_copy(k, col).wait_send()
        out_copy(k, k).wait_recv()


def shards(markers):
    sem = pltpu.SemaphoreType.DMA
    return pl.pallas_call(
        kernel,
        out_shape=jax.ShapeDtypeStruct((BK, 1024), F32),
        in_specs=[pl.BlockSpec(memory_space=pl.ANY)],
        out_specs=pl.BlockSpec(memory_space=pltpu.VMEM),
        scratch_shapes=[
            pltpu.VMEM((1024, 2048), BF16),
            pltpu.VMEM((PANEL, 2048), BF16),
            pltpu.VMEM((PANEL, PANEL), F32),
            pltpu.VMEM((PANEL, PANEL), F32),
            pltpu.VMEM((PB, PANEL), F32),
            pltpu.VMEM((NB, PB, BK), F32),
            pltpu.VMEM((PB, BK), F32),
            pltpu.VMEM((NB, NB, BK, BK), F32),
            pltpu.VMEM((NB, 5, BK, BK), F32),
            pltpu.VMEM((NB, 2, BK, BK), F32),
            pltpu.VMEM((PANEL, BK), F32),
            pltpu.VMEM((PANEL, BK), F32),
            pltpu.VMEM((BK, BK), F32),
            pltpu.VMEM((PANEL, 6 * BK), BF16),
            pltpu.VMEM((PANEL, 6 * BK), BF16),
            pltpu.VMEM((BK, 6 * BK), BF16),
            pltpu.VMEM((BK, 6 * BK), BF16),
            sem((2,)), sem((16 + 17 * PARTS,)), sem((16 + 17 * PARTS,)), sem((16 + 17 * PARTS,)), sem((16 + 17 * PARTS,)),
            sem((NB,)), sem((NB,)), sem((NB,)), sem((NB,)),
            sem((5 * NB,)), sem((5 * NB,)), sem((NB,)), sem((NB,)),
        ],
        compiler_params=pltpu.CompilerParams(
            collective_id=0, has_side_effects=True, vmem_limit_bytes=58 * 1024 * 1024
        ),
    )(markers)


def solution(mesh):
    return jax.shard_map(
        shards, mesh=mesh, in_specs=(P("row", "col"),), out_specs=P("col", "row"), check_vma=False
    )
```

```python
import functools

import jax
import jax.numpy as jnp
from jax import lax
from jax.experimental import pallas as pl
from jax.experimental.pallas import tpu as pltpu
from jax.sharding import PartitionSpec as P

M = 16384
PANEL = 1024
PB = 32
NB = 8
BK = 128
RIDGE = 0.001
PARTS = 1
KEPT = 5
MESH = pl.DeviceIdType.MESH
F32 = jnp.float32
BF16 = jnp.bfloat16


def split3(x):
    high = x.astype(BF16)
    rest = x - high.astype(F32)
    mid = rest.astype(BF16)
    low = (rest - mid.astype(F32)).astype(BF16)
    return high, mid, low


def stack_left(x, axis=1):
    high, mid, low = split3(x)
    return jnp.concatenate([high, high, high, mid, mid, low], axis=axis)


def stack_right(x, axis=1):
    high, mid, low = split3(x)
    return jnp.concatenate([high, mid, low, high, mid, high], axis=axis)


def dot_nt(a, b):
    return lax.dot_general(a, b, (((1,), (1,)), ((), ())), preferred_element_type=F32)


def dot_nn(a, b):
    return lax.dot_general(a, b, (((1,), (0,)), ((), ())), preferred_element_type=F32)


def recip(x):
    return pltpu.reciprocal(x, approx=True)


def row_of(x, i):
    return jnp.broadcast_to(x[i : i + 1, :], (8, BK))


def col_of(x, j):
    return jnp.broadcast_to(x[:, j : j + 1], (8, BK))


def factor8(c):
    w = [[None] * 8 for _ in range(8)]
    rp = [None] * 8
    for i in range(8):
        w[i][i] = jnp.ones_like(c[0][0])
    for s in range(8):
        rp[s] = recip(c[s][s])
        for i in range(s + 1, 8):
            f = c[i][s] * rp[s]
            for j in range(s + 1, i + 1):
                c[i][j] = c[i][j] - f * c[j][s]
            for q in range(s):
                w[i][q] = w[i][q] - f * w[s][q]
            w[i][s] = -f
    return w, rp


def factor_inverse(a):
    tiles = [a[8 * t : 8 * t + 8, :] for t in range(16)]
    lane = lax.broadcasted_iota(jnp.int32, (8, BK), 1)
    sub = lax.broadcasted_iota(jnp.int32, (8, BK), 0)
    out, scaled, plain = [], [], []
    cols = None
    for t in range(16):
        x, b0 = tiles[t], 8 * t
        end = 8 if t < 8 else 16
        if cols is None:
            cols = [col_of(x, b0 + j) for j in range(8)]
        w, rp = factor8([[row_of(cols[j], i) for j in range(i + 1)] for i in range(8)])
        inside = (lane >= b0) & (lane < b0 + 8)

        def multipliers(i):
            e = [col_of(tiles[i], b0 + j) for j in range(8)]
            g = []
            for s in range(8):
                f = e[s]
                for j in range(s):
                    f = f + w[s][j] * e[j]
                g.append(f)
            return g

        cols = None
        if t + 1 < end:
            g = multipliers(t + 1)
            f = [g[s] * rp[s] for s in range(8)]
            cols = [col_of(tiles[t + 1], b0 + 8 + j) for j in range(8)]
            for s in range(8):
                cols = [cols[j] - f[s] * row_of(g[s], j) for j in range(8)]
        xt = jnp.where(inside, (lane - b0 == sub).astype(F32), x)
        r = [row_of(xt, i) for i in range(8)]
        u = []
        for s in range(8):
            y = r[s]
            for j in range(s):
                y = y + w[s][j] * r[j]
            u.append(y)
        y, p = u[0], rp[0]
        for s in range(1, 8):
            y = jnp.where(sub == s, u[s], y)
            p = jnp.where(sub == s, rp[s], p)
        below = lane <= b0 + sub
        out.append(jnp.where(below, y * lax.sqrt(p), 0.0))
        for i in range(t + 1, end):
            if i > t + 1:
                f = [h * q for h, q in zip(multipliers(i), rp)]
            z = jnp.where(inside, 0.0, tiles[i])
            for s in range(8):
                z = z - f[s] * u[s]
            tiles[i] = z
        if t < 8:
            scaled.append(y * p)
            plain.append(jnp.where(below | (lane >= 64), y, 0.0))
        if t == 7:
            lh, lm, ll = (x.astype(F32) for x in split3(jnp.concatenate(scaled, axis=0)))
            rh, rm, rl = split3(jnp.concatenate(plain, axis=0))
            half = jnp.where(lax.broadcasted_iota(jnp.int32, (64, BK), 1) < 64, 0.0, jnp.concatenate(tiles[8:], axis=0))
            for left, right in (((lh, lm), (rl, rh)), ((lm, ll), (rm, rh)), ((lh, lh), (rh, rm))):
                turned = jnp.transpose(jnp.concatenate(left, axis=0))[64:, :].astype(BF16)
                half = half - dot_nn(turned, jnp.concatenate(right, axis=0))
            tiles[8:] = [half[8 * i : 8 * i + 8, :] for i in range(8)]
    return jnp.concatenate(out, axis=0)


def block_at(k):
    return pl.ds(pl.multiple_of(k * BK, BK), BK)


def factor_steps(a_ref, g_ref, diag, left_ref, right_ref, invl_ref, invr_ref, at_first, emit):
    diag[...] = a_ref[:BK, :BK]
    invl_ref[...] = jnp.zeros_like(invl_ref)
    invr_ref[...] = jnp.zeros_like(invr_ref)

    def step(base, k, carry):
        here = block_at(k)
        before = block_at(jnp.maximum(k - 1, 0))
        after = block_at(jnp.minimum(k + 1, NB - 1))
        block = diag[...]

        if base == 0:
            @pl.when(k == 1)
            def _():
                at_first()

        s_k = dot_nn(invl_ref[...], stack_right(g_ref[before, :], axis=0))
        panel = dot_nt(stack_left(a_ref[base:, before]), invr_ref[...])
        rows = lax.broadcasted_iota(jnp.int32, (PANEL - base, BK), 0) + base
        panel = jnp.where(rows >= k * BK, panel, 0.0)
        left_ref[base:, :] = stack_left(panel)
        right_ref[base:, :] = stack_right(panel)
        for j in range(base // (2 * BK), NB // 2):
            cols = slice(2 * BK * j, 2 * BK * (j + 1))
            top = 0 if j < NB // 4 else PANEL // 2
            a_ref[top:, cols] -= dot_nt(left_ref[top:, :], right_ref[cols, :])
        g_ref[base:, :] -= dot_nn(left_ref[base:, :], stack_right(s_k, axis=0))
        inverse = factor_inverse(block)
        inv_r = stack_right(inverse)
        invl_ref[...] = stack_left(inverse)
        invr_ref[...] = inv_r
        low = dot_nt(stack_left(a_ref[after, here]), inv_r)
        diag[...] = a_ref[after, after] - dot_nt(stack_left(low), stack_right(low))
        emit(k - 1, s_k)
        return carry

    lax.fori_loop(0, NB // 2, functools.partial(step, 0), 0)
    lax.fori_loop(NB // 2, NB, functools.partial(step, PANEL // 2), 0)
    last = slice(PANEL - BK, PANEL)
    emit(NB - 1, dot_nn(invl_ref[...], stack_right(g_ref[last, :], axis=0)))


def kernel(
    markers_ref, out_ref,
    own, panel, a_ref, turned, dpart, drecv, dred, gsend, grecv, relay, g_ref, solved, diag, left_ref, right_ref, invl_ref, invr_ref,
    local_sem, ag_send, ag_recv, dag_send, dag_recv, rs_send, rs_recv, dc_send, dc_recv,
    gs_send, gs_recv, os_send, os_recv,
):
    row = lax.axis_index("row")
    col = lax.axis_index("col")
    core = lax.rem(row, 2)
    z = lax.rem(row // 2, 8)
    hi = row // 16

    def row_id(h, zz, q):
        return h * 16 + zz * 2 + q

    sibling = row_id(hi, z, 1 - core)
    partner = row_id(1 - hi, z, core)
    up = row_id(hi, lax.rem(z + 1, 8), core)
    down = row_id(hi, lax.rem(z + 7, 8), core)
    up2 = row_id(hi, lax.rem(z + 2, 8), core)
    down2 = row_id(hi, lax.rem(z + 6, 8), core)
    row_peers = (sibling, partner, up, down, up2, down2)
    col_peers = [lax.rem(col + o, NB) for o in range(1, NB)]

    load_panel = pltpu.make_async_copy(
        markers_ref.at[pl.ds(0, PB), :], panel.at[pl.ds(pl.multiple_of(row * PB, PB), PB), :], local_sem.at[0]
    )
    load_panel.start()
    load_own = pltpu.make_async_copy(markers_ref, own, local_sem.at[1])
    load_own.start()

    barrier = pltpu.get_barrier_semaphore()
    for peer in row_peers:
        pl.semaphore_signal(barrier, inc=1, device_id=(peer, col), device_id_type=MESH)
    for peer in col_peers:
        pl.semaphore_signal(barrier, inc=1, device_id=(row, peer), device_id_type=MESH)
    pl.semaphore_wait(barrier, len(row_peers) + len(col_peers))

    def piece_id(h, zz):
        return h * 8 + zz

    def gather(buf, width, skip, send, recv, between):
        size = PB // PARTS

        def rows_of(r, part):
            if part is None:
                return buf.at[pl.ds(pl.multiple_of(r * PB, PB), PB), pl.ds(0, width)]
            return buf.at[pl.ds(pl.multiple_of(r * PB + part * size, size), size), pl.ds(0, width)]

        started = []

        def copy(r, part, target, index, go=True):
            c = pltpu.make_async_remote_copy(
                src_ref=rows_of(r, part), dst_ref=rows_of(r, part), send_sem=send.at[index], recv_sem=recv.at[index],
                device_id=(target, col), device_id_type=MESH,
            )
            if go:
                c.start()
                started.append(c)
            return c

        def index_of(stream, way, d, part):
            return 16 + PARTS + ((stream * 2 + way) * 4 + d - 1) * PARTS + part

        def source(stream, way, d):
            h = hi if stream == 0 else 1 - hi
            zz = lax.rem(z + (8 - d if way == 0 else d), 8)
            return row_id(h, zz, core)

        def forward(stream, way, d, part):
            copy(source(stream, way, d), part, up if way == 0 else down, index_of(stream, way, d + 1, part))

        reach = {(0, 0): 4, (0, 1): 3, (1, 0): 3, (1, 1): 4}
        sib_done = []

        def to_sibling(r, index):
            copy(r, None, sibling, index)
            sib_done.append(copy(r + 1 - 2 * core, None, sibling, index, go=False))

        def from_sibling():
            for c in sib_done:
                c.wait_recv()
            sib_done.clear()

        for part in range(PARTS):
            copy(row, part, partner, 16 + part)
            forward(0, 0, 0, part)
            forward(0, 1, 0, part)
        to_sibling(row, 0)
        for part in range(PARTS):
            copy(partner, part, partner, 16 + part, go=False).wait_recv()
            forward(1, 0, 0, part)
            forward(1, 1, 0, part)
        to_sibling(partner, 1)
        n = 2
        for d in range(1, 5):
            ways = [sw for sw in ((0, 0), (0, 1), (1, 0), (1, 1)) if d <= reach[sw]]
            for part in range(PARTS):
                for stream, way in ways:
                    copy(source(stream, way, d), part, sibling, index_of(stream, way, d, part), go=False).wait_recv()
                    if d < (min(3, reach[stream, way]) if skip else reach[stream, way]):
                        forward(stream, way, d, part)
                    if skip and d == 2 and reach[stream, way] == 4:
                        far = up2 if way == 0 else down2
                        copy(source(stream, way, d), part, far, index_of(stream, way, 4, part))
            from_sibling()
            for stream, way in ways:
                to_sibling(source(stream, way, d), n)
                n += 1
            between(d)
        from_sibling()
        return started

    def pieces(d):
        if d == 0:
            return [piece_id(hi, z), piece_id(1 - hi, z)]
        plus, minus = lax.rem(z + 8 - d, 8), lax.rem(z + d, 8)
        if d == 4:
            return [piece_id(hi, plus), piece_id(1 - hi, plus)]
        return [piece_id(hi, plus), piece_id(hi, minus), piece_id(1 - hi, plus), piece_id(1 - hi, minus)]

    first_tile = [0, 1, 3, 5, 7]
    gram_copies = []

    def col_at(dx, dy):
        return lax.rem(col // 2 + dx, 4) * 2 + lax.rem(col + dy, 2)

    direct = [(0, 1), (1, 1), (3, 0), (1, 0), (3, 1)]

    def sums_copy(d, slot, target, buf, index, sem):
        t0, tiles = first_tile[d], len(pieces(d)) // 2
        c = pltpu.make_async_remote_copy(
            src_ref=gsend.at[pl.ds(t0, tiles), slot], dst_ref=buf.at[pl.ds(t0, tiles), index],
            send_sem=gs_send.at[d * NB + sem], recv_sem=gs_recv.at[d * NB + sem],
            device_id=(row, target), device_id_type=MESH,
        )
        c.start()
        return c

    def direct_copy(d, index):
        dx, dy = direct[index]
        gram_copies.append(sums_copy(d, dx * 2 + dy, col_at(dx, dy), grecv, index, index))

    relays = {}

    def gram_chunk(d):
        ids = pieces(d)
        t0 = first_tile[d]
        chosen = jnp.concatenate([panel[pl.ds(pl.multiple_of(p * 64, 64), 64), :] for p in ids], axis=0)
        sums = dot_nt(own[...], chosen)
        for dest in range(NB):
            slot = lax.rem(dest // 2 + 4 - col // 2, 4) * 2 + lax.rem(dest % 2 + 2 - lax.rem(col, 2), 2)
            for t in range(len(ids) // 2):
                gsend[t0 + t, slot] = sums[dest * BK : (dest + 1) * BK, t * BK : (t + 1) * BK]

    def gram_send(d):
        relays[d] = [
            sums_copy(d, 4, col_at(1, 0), relay, 0, 5),
            sums_copy(d, 5, col_at(3, 0), relay, 1, 6),
        ]
        for index in range(3):
            direct_copy(d, index)

    def gram_relay(d):
        for c in relays[d]:
            c.wait_recv()
        for t in range(first_tile[d], first_tile[d] + len(pieces(d)) // 2):
            gsend[t, 2] += relay[t, 0]
            gsend[t, 7] += relay[t, 1]
        for index in (3, 4):
            direct_copy(d, index)

    load_panel.wait()

    def while_gathering(d):
        if d == 1:
            load_own.wait()
            a_ref[...] = jnp.zeros_like(a_ref)
            g_ref[...] = jnp.zeros_like(g_ref)
        if d < 4:
            gram_chunk(d - 1)
            gram_send(d - 1)
        if d in (2, 3):
            gram_relay(d - 2)

    started = gather(panel, 2048, False, ag_send, ag_recv, while_gathering)

    mine = pl.ds(pl.multiple_of(row * PB, PB), PB)
    here = pl.ds(pl.multiple_of(col * BK, BK), BK)
    dpart[...] = dot_nt(panel[mine, :], panel[...])

    def reduce_copy(o, target):
        return pltpu.make_async_remote_copy(
            src_ref=dpart.at[:, pl.ds(pl.multiple_of(target * BK, BK), BK)], dst_ref=drecv.at[o],
            send_sem=rs_send.at[o], recv_sem=rs_recv.at[o], device_id=(row, target), device_id_type=MESH,
        )

    scatter = [reduce_copy(o, col_peers[o - 1]) for o in range(1, NB)]
    for c in scatter:
        c.start()
    gram_chunk(3)
    for c in scatter:
        c.wait_recv()
    total = dpart[:, here]
    for o in range(1, NB):
        total = total + drecv[o]
    diagonal = (
        lax.broadcasted_iota(jnp.int32, (PB, BK), 0) + row * PB
        == lax.broadcasted_iota(jnp.int32, (PB, BK), 1) + col * BK
    )
    dred[...] = total * (1.0 / M) + jnp.where(diagonal, RIDGE, 0.0)
    kept = block_at(lax.rem(col + NB + KEPT - 1 - row // 4, NB))
    turned[mine, kept] = dred[...]

    def spread_copy(o, target):
        return pltpu.make_async_remote_copy(
            src_ref=dred, dst_ref=turned.at[mine, kept],
            send_sem=dc_send.at[o], recv_sem=dc_recv.at[o], device_id=(row, target), device_id_type=MESH,
        )

    spread = [spread_copy(o, col_peers[o - 1]) for o in range(1, NB)]
    for c in spread:
        c.start()
    gram_chunk(4)
    for c in spread:
        c.wait_recv()

    def while_spreading(d):
        if d == 1:
            gram_send(3)
            gram_send(4)
            gram_relay(2)
        elif d == 3:
            gram_relay(3)
            gram_relay(4)

    started += gather(turned, KEPT * BK, True, dag_send, dag_recv, while_spreading)
    for i in range(NB):
        for j in range(i + 1):
            m = (j - i + KEPT - 1) % NB
            if m < KEPT:
                a_ref[i * BK : (i + 1) * BK, j * BK : (j + 1) * BK] = turned[i * BK : (i + 1) * BK, m * BK : (m + 1) * BK]
            else:
                m = (i - j + KEPT - 1) % NB
                a_ref[i * BK : (i + 1) * BK, j * BK : (j + 1) * BK] = jnp.transpose(
                    turned[j * BK : (j + 1) * BK, m * BK : (m + 1) * BK]
                )

    def sum_gram():
        for c in gram_copies:
            c.wait_recv()
        for d in range(5):
            ids = pieces(d)
            for t in range(len(ids) // 2):
                tile = first_tile[d] + t
                total = gsend[tile, 0]
                for s in range(len(direct)):
                    total = total + grecv[tile, s]
                total = jnp.transpose(total) * (1.0 / M)
                for half in range(2):
                    rows = pl.ds(pl.multiple_of(ids[2 * t + half] * 64, 64), 64)
                    g_ref[rows, :] = total[half * 64 : half * 64 + 64, :]
        ridge = (
            (lax.broadcasted_iota(jnp.int32, (PB, BK), 0) == lax.broadcasted_iota(jnp.int32, (PB, BK), 1))
            & (col == 0)
        )
        g_ref[mine, :] += jnp.where(ridge, RIDGE, 0.0)

    def out_copy(k, source):
        return pltpu.make_async_remote_copy(
            src_ref=solved.at[block_at(k), :], dst_ref=out_ref.at[:, pl.ds(pl.multiple_of(source * BK, BK), BK)],
            send_sem=os_send.at[k], recv_sem=os_recv.at[source], device_id=(row, k), device_id_type=MESH,
        )

    def emit(k, rows):
        solved[block_at(jnp.maximum(k, 0)), :] = rows

        @pl.when((k >= 0) & (col != k))
        def _():
            out_copy(k, col).start()

    factor_steps(a_ref, g_ref, diag, left_ref, right_ref, invl_ref, invr_ref, sum_gram, emit)
    for c in started + scatter + spread + gram_copies:
        c.wait_send()
    for pair in relays.values():
        for c in pair:
            c.wait_send()
    keep = pltpu.make_async_copy(solved.at[here, :], out_ref.at[:, here], local_sem.at[0])
    keep.start()
    for o in range(1, NB):
        k = col_peers[o - 1]
        out_copy(k, col).wait_send()
        out_copy(k, k).wait_recv()
    keep.wait()


def shards(markers):
    sem = pltpu.SemaphoreType.DMA
    return pl.pallas_call(
        kernel,
        out_shape=jax.ShapeDtypeStruct((BK, 1024), F32),
        in_specs=[pl.BlockSpec(memory_space=pl.ANY)],
        out_specs=pl.BlockSpec(memory_space=pl.ANY),
        scratch_shapes=[
            pltpu.VMEM((1024, 2048), BF16),
            pltpu.VMEM((PANEL, 2048), BF16),
            pltpu.VMEM((PANEL, PANEL), F32),
            pltpu.VMEM((PANEL, PANEL), F32),
            pltpu.VMEM((PB, PANEL), F32),
            pltpu.VMEM((NB, PB, BK), F32),
            pltpu.VMEM((PB, BK), F32),
            pltpu.VMEM((NB, NB, BK, BK), F32),
            pltpu.VMEM((NB, 5, BK, BK), F32),
            pltpu.VMEM((NB, 2, BK, BK), F32),
            pltpu.VMEM((PANEL, BK), F32),
            pltpu.VMEM((PANEL, BK), F32),
            pltpu.VMEM((BK, BK), F32),
            pltpu.VMEM((PANEL, 6 * BK), BF16),
            pltpu.VMEM((PANEL, 6 * BK), BF16),
            pltpu.VMEM((BK, 6 * BK), BF16),
            pltpu.VMEM((BK, 6 * BK), BF16),
            sem((2,)), sem((16 + 17 * PARTS,)), sem((16 + 17 * PARTS,)), sem((16 + 17 * PARTS,)), sem((16 + 17 * PARTS,)),
            sem((NB,)), sem((NB,)), sem((NB,)), sem((NB,)),
            sem((5 * NB,)), sem((5 * NB,)), sem((NB,)), sem((NB,)),
        ],
        compiler_params=pltpu.CompilerParams(
            collective_id=0, has_side_effects=True, vmem_limit_bytes=58 * 1024 * 1024
        ),
    )(markers)


def solution(mesh):
    return jax.shard_map(
        shards, mesh=mesh, in_specs=(P("row", "col"),), out_specs=P("col", "row"), check_vma=False
    )
```
